128 devices in a mesh: grp: 4 (over z), sub: 32 (over y, x, core).
Axes of the slice: x: 4, y: 4, z: 4, core: 2. Of those that a mesh axis runs over, the one named last changes fastest.
Arguments:
- loads: float32 [512, 8, 32, 128], P(('grp', 'sub')), may hold values from -20 to 20
- schur: bfloat16 [512, 1024, 1024], P(('grp', 'sub')), may hold values from 0 to 8, as said below
- local_inverse: bfloat16 [512, 1024, 1024], P(('grp', 'sub')), may hold values from 0 to 1, as said below
- coarse_basis: float32 [512, 8, 8, 128], P(('grp', 'sub')), may hold values from -0.375 to 0.375
- coarse_inverse: float32 [2048, 2048], P('sub'), may hold values from 0 to 1, as said below
- primal_index: int32 [512, 8], P(('grp', 'sub')), may hold values from 0 to 2047
- nbr_sub: int32 [512, 8], P(('grp', 'sub')), may hold values from -1 to 511, as said below
- nbr_block: int32 [512, 8], P(('grp', 'sub')), may hold values from -1 to 7, as said below
Outputs:
- solution: float32 [512, 8, 32, 128], P(('grp', 'sub'))
- precond: float32 [512, 8, 32, 128], P(('grp', 'sub'))
The draws below stay inside these ranges and needn't reach their ends.
Inputs may be any that keep to these rules, and one draw needn't show every extreme that they name: `nbr_sub`: for a face b < 6, the partner subdomain lies on another device with the same grp index, and its entry names this face back. No device has more than 2 such faces whose partners lie on one other device; some pair of devices has exactly 2. Face 8 - 2 of a subdomain pairs with face 8 - 1 of the subdomain at the same place on the device with the next grp index and the same sub index, face 8 - 1 with face 8 - 2 on the device with the previous grp index; none (-1) at the first and last grp index. `nbr_block`: the partner's face index, -1 where there is no partner. `schur`: each subdomain's matrix is symmetric positive definite. `local_inverse`: each subdomain's matrix is symmetric positive definite. `coarse_inverse`: symmetric positive definite.
All inputs are finite; a program needn't handle non-finite values.
Results may differ from the reference program's by a relative error of at most 0.0026.
Values sent between devices are 32-bit elements; how exact they have to be, the bound alone decides.
No kernel may reach another device: no remote copies, remote signals or barrier semaphores. Data moves between devices by JAX's collectives and lax.ppermute only.
A program may use at most 128 MiB of HBM per device.

```python
import jax
import jax.numpy as jnp
import numpy as np
from jax import lax

NI = 1024
NB = 8
BW = 128
SUB_DEV = 4
NRHS = 32
NC = 8
ITERS = 2
NSUB = 512
NPRIM = 2048
CAP = 2
N_GRP = 4
N_SUB = 32


def kernel_matrix(points, amplitude, diagonal):
    distance = jnp.abs(points[:, None] - points[None, :])
    identity = jnp.eye(points.shape[0], dtype=jnp.float32)
    return diagonal[:, None] * identity + amplitude[:, None] * amplitude[None, :] * jnp.exp(-distance)


def stiffness(key):
    return jnp.exp(jax.random.uniform(key, (NSUB,), jnp.float32, 0.0, jnp.log(10.0)))


def subdomain_blocks(key, factors, lowest):

    def single(operands):
        sub_key, factor = operands
        key_points, key_scale, key_diagonal = jax.random.split(sub_key, 3)
        points = jax.random.uniform(key_points, (NI,), jnp.float32, 0.0, NI / 4.0)
        amplitude = jax.random.uniform(key_scale, (NI,), jnp.float32, lowest, 1.0)
        diagonal = jax.random.uniform(key_diagonal, (NI,), jnp.float32, 1.0, 2.0)
        return (0.25 * factor * kernel_matrix(points, amplitude, diagonal)).astype(jnp.bfloat16)
    return lax.map(single, (jax.random.split(key, NSUB), factors))


def draw_schur(key, part):
    factors = stiffness(key)
    key = jax.random.fold_in(key, 3)
    lowest = 0.5
    return subdomain_blocks(key, factors, lowest)


def draw_local_inverse(key, part):
    factors = 1.0 / stiffness(key)
    key = jax.random.fold_in(key, 4)
    lowest = 0.5
    return subdomain_blocks(key, factors, lowest)


def draw_coarse_inverse(key, part):
    key = jax.random.fold_in(key, 5)
    key_points, key_scale, key_diagonal = jax.random.split(key, 3)
    lowest = 0.5
    points = jax.random.uniform(key_points, (NPRIM,), jnp.float32, 0.0, NPRIM / 8.0)
    amplitude = jax.random.uniform(key_scale, (NPRIM,), jnp.float32, lowest, 1.0)
    diagonal = jax.random.uniform(key_diagonal, (NPRIM,), jnp.float32, 0.5, 1.0)
    return 0.25 * kernel_matrix(points, amplitude, diagonal)


def draw_loads(key, part):
    key = jax.random.fold_in(key, 7)
    full_shape = (NSUB, NB, NRHS, NI // NB)
    ramp = jnp.arange(NSUB, dtype=jnp.float32) / max(NSUB - 1, 1)
    rising = jnp.exp(jnp.log(3.0) * ramp)
    values = jnp.clip(jax.random.normal(key, full_shape, jnp.float32), -6.0, 6.0)
    return rising[:, None, None, None] * values


def neighbour_lists(key):
    face_count = NB - 2
    slot_count = SUB_DEV * face_count
    heavy = min(slot_count // CAP, max(1, -((N_SUB - 1 - slot_count) // (CAP - 1))))
    slots = np.arange(slot_count)
    grouped = slots < CAP * heavy
    mask_slot = np.where(grouped, slots // CAP, heavy + slots - CAP * heavy)
    offset = slots % CAP
    flipped = offset ^ 1
    swapped = slots // CAP * CAP + flipped
    partner_slot = np.where(grouped & (flipped < CAP), swapped, slots)
    key_masks, key_places = jax.random.split(key)
    mask_order = jax.vmap(lambda sub_key: jax.random.permutation(sub_key, N_SUB - 1) + 1)(jax.random.split(key_masks, N_GRP))
    placement = jax.vmap(lambda sub_key: jax.random.permutation(sub_key, slot_count))(jax.random.split(key_places, N_GRP * N_SUB))
    placement = placement.reshape(N_GRP, N_SUB, slot_count).astype(jnp.int32)
    slot_of = jnp.argsort(placement, axis=-1).astype(jnp.int32)
    masks = mask_order[:, mask_slot].astype(jnp.int32)
    group_ids = jnp.arange(N_GRP, dtype=jnp.int32)[:, None, None]
    device_ids = jnp.arange(N_SUB, dtype=jnp.int32)[None, :, None]
    chosen_mask = jnp.take_along_axis(jnp.broadcast_to(masks[:, None, :], placement.shape), slot_of, axis=2)
    partner_device = device_ids ^ chosen_mask
    partner_slots = jnp.asarray(partner_slot, dtype=jnp.int32)[slot_of]
    partner_place = placement[group_ids, partner_device, partner_slots]
    partner_sub = (group_ids * N_SUB + partner_device) * SUB_DEV + partner_place // face_count
    partner_face = partner_place % face_count
    stride = N_SUB * SUB_DEV
    owners = jnp.arange(NSUB, dtype=jnp.int32)
    group_of = owners // stride
    upper_sub = jnp.where(group_of < N_GRP - 1, owners + stride, -1)
    lower_sub = jnp.where(group_of > 0, owners - stride, -1)
    upper_face = jnp.where(group_of < N_GRP - 1, NB - 1, -1)
    lower_face = jnp.where(group_of > 0, NB - 2, -1)
    subs = jnp.concatenate([partner_sub.reshape(NSUB, face_count), upper_sub[:, None], lower_sub[:, None]], axis=1)
    faces = jnp.concatenate([partner_face.reshape(NSUB, face_count), upper_face[:, None], lower_face[:, None]], axis=1)
    return (subs.astype(jnp.int32), faces.astype(jnp.int32))


def draw_nbr_sub(key, part):
    return neighbour_lists(key)[0]


def draw_nbr_block(key, part):
    return neighbour_lists(key)[1]


def touch_ends(entries, own_key, least, largest):
    longest = entries.shape.index(max(entries.shape))
    spots = []
    for shift in (0, 1):
        where = [jax.random.randint(jax.random.fold_in(own_key, axis), (), 0, length) for axis, length in enumerate(entries.shape)]
        where[longest] = (where[longest] + shift) % entries.shape[longest]
        spots.append(tuple(where))
    return entries.at[spots[0]].set(least).at[spots[1]].set(largest)


def shard_levels(own_key, dims, shards, least, largest):
    loudness = 1.0
    for position, parts in shards:
        draws = jax.random.uniform(jax.random.fold_in(jax.random.fold_in(own_key, 6), position), (parts,), jnp.float32, least / len(shards), largest / len(shards))
        loudness = loudness * jnp.repeat(jnp.exp(draws), dims[position] // parts).reshape((-1,) + (1,) * (len(dims) - 1 - position))
    return loudness


def scatter_about(stream_key, extent, spread, reach, cuts=(), held_as=jnp.bfloat16):
    entries = jax.random.normal(stream_key, extent, jnp.float32) * spread
    if len(cuts) > 0:
        entries = shard_levels(stream_key, extent, cuts, -0.22, 0.18) * entries
    return jnp.clip(entries, min=-reach, max=reach).astype(held_as)


def setup_inputs(seed: int = 0) -> dict:
    splits = jax.random.split(jax.random.key(seed), 9)
    loads = draw_loads(jax.random.fold_in(splits[8], 71), 0)
    schur = draw_schur(jax.random.fold_in(splits[8], 71), 0)
    local_inverse = draw_local_inverse(jax.random.fold_in(splits[8], 71), 0)
    coarse_basis = scatter_about(splits[3], (NSUB, NC, NB, BW), (NI // 4) ** -0.5, 0.375, ((0, 128),), jnp.float32)
    coarse_inverse = draw_coarse_inverse(jax.random.fold_in(splits[8], 71), 0)
    primal_index = touch_ends(jax.random.randint(splits[5], (NSUB, NC), 0, NPRIM), jax.random.fold_in(splits[5], 1), 0, NPRIM - 1).astype(jnp.int32)
    nbr_sub = draw_nbr_sub(jax.random.fold_in(splits[8], 71), 0)
    nbr_block = draw_nbr_block(jax.random.fold_in(splits[8], 71), 0)
    return dict(loads=loads, schur=schur, local_inverse=local_inverse, coarse_basis=coarse_basis, coarse_inverse=coarse_inverse, primal_index=primal_index, nbr_sub=nbr_sub, nbr_block=nbr_block)


PRECISE = lax.Precision.HIGHEST


def apply_blocks(matrices, field):
    def single(operands):
        matrix, vector = operands
        flattened = vector.astype(jnp.bfloat16).transpose(1, 0, 2).reshape(vector.shape[1], vector.shape[0] * vector.shape[2])
        product = jnp.dot(flattened, matrix, preferred_element_type=jnp.float32)
        return product.reshape(vector.shape[1], vector.shape[0], vector.shape[2]).transpose(1, 0, 2)
    return lax.map(single, (matrices, field))


def assemble(field, nbr_sub, nbr_block):
    paired = nbr_sub >= 0
    partner_vals = field[jnp.maximum(nbr_sub, 0), jnp.maximum(nbr_block, 0)]
    return field + jnp.where(paired[:, :, None, None], partner_vals, jnp.zeros_like(partner_vals))


def precondition(resid, weights, local_inverse, coarse_basis, coarse_inverse, primal_index, nbr_sub, nbr_block):
    weighted = weights * resid
    local_part = apply_blocks(local_inverse, weighted)
    projected = jnp.einsum('scbk,sbrk->scr', coarse_basis, weighted, precision=PRECISE)
    coarse_total = jax.ops.segment_sum(projected.reshape(-1, projected.shape[-1]), primal_index.reshape(-1), num_segments=NPRIM)
    coarse_values = jnp.dot(coarse_inverse, coarse_total, precision=PRECISE)
    picked = coarse_values[primal_index]
    corrected = local_part + jnp.einsum('scbk,scr->sbrk', coarse_basis, picked, precision=PRECISE)
    return assemble(weights * corrected, nbr_sub, nbr_block)


def reference(loads, schur, local_inverse, coarse_basis, coarse_inverse, primal_index, nbr_sub, nbr_block):
    weights = (1.0 / (1.0 + (nbr_sub >= 0).astype(jnp.float32)))[:, :, None, None]
    resid = assemble(loads, nbr_sub, nbr_block)
    precond = precondition(resid, weights, local_inverse, coarse_basis, coarse_inverse, primal_index, nbr_sub, nbr_block)
    resid_dot = jnp.sum(weights * resid * precond, axis=(0, 1, 3))
    direction = precond
    solution = jnp.zeros_like(loads)
    for iteration in range(ITERS):
        product = apply_blocks(schur, direction)
        curvature = jnp.sum(direction * product, axis=(0, 1, 3))
        image = assemble(product, nbr_sub, nbr_block)
        step_size = (resid_dot / curvature)[None, None, :, None]
        solution = solution + step_size * direction
        resid = resid - step_size * image
        precond = precondition(resid, weights, local_inverse, coarse_basis, coarse_inverse, primal_index, nbr_sub, nbr_block)
        if iteration + 1 < ITERS:
            dot_next = jnp.sum(weights * resid * precond, axis=(0, 1, 3))
            direction = precond + (dot_next / resid_dot)[None, None, :, None] * direction
            resid_dot = dot_next
    return solution, precond
```

```python
import jax
import jax.numpy as jnp
from jax import lax
from jax.sharding import PartitionSpec as P

AXES = ("grp", "sub")
PRECISE = lax.Precision.HIGHEST


def face_routes(nbr_sub, nbr_block, peer_count, capacity):
    sub_here = nbr_sub.shape[0]
    face_count = nbr_sub.shape[1] - 2
    partner = nbr_sub[:, :face_count].reshape(-1)
    peer_index = partner // sub_here % peer_count
    partner_place = partner % sub_here * face_count + nbr_block[:, :face_count].reshape(-1)
    places = jnp.arange(sub_here * face_count, dtype=jnp.int32)
    same_peer = peer_index[:, None] == peer_index[None, :]
    send_rank = jnp.sum(same_peer & (places[None, :] < places[:, None]), axis=1)
    recv_rank = jnp.sum(same_peer & (partner_place[None, :] < partner_place[:, None]), axis=1)
    send_slot = peer_index * capacity + send_rank
    recv_slot = peer_index * capacity + recv_rank
    slot_ids = jnp.arange(peer_count * capacity, dtype=jnp.int32)
    matches = slot_ids[:, None] == send_slot[None, :]
    source = jnp.sum(jnp.where(matches, places[None, :], 0), axis=1)
    filled = jnp.any(matches, axis=1)
    return (source, filled, recv_slot)


def all_to_all(block, axes):
    return lax.all_to_all(block, axes, split_axis=0, concat_axis=0, tiled=True)


def assemble(partial_sum, routes, rider=None):
    source, filled, recv_slot = routes
    sub_here, blocks, case_count, block_width = partial_sum.shape
    face_count = blocks - 2
    peers = lax.axis_size("sub")
    shared = partial_sum[:, :face_count].reshape(sub_here * face_count, case_count, block_width)
    outgoing = jnp.where(filled[:, None, None], shared[source], 0.0)
    slots = outgoing.shape[0] // peers
    outgoing = outgoing.reshape(peers, slots * case_count, block_width)
    if rider is not None:
        outgoing = jnp.concatenate([outgoing, rider], axis=1)
    incoming = all_to_all(outgoing, "sub")
    landed = incoming[:, slots * case_count :]
    incoming = incoming[:, : slots * case_count].reshape(peers * slots, case_count, block_width)
    devices = lax.axis_size("grp")
    up = [(i, i + 1) for i in range(devices - 1)]
    down = [(j, i) for i, j in up]
    before = lax.ppermute(partial_sum[:, blocks - 2], "grp", up)
    after = lax.ppermute(partial_sum[:, blocks - 1], "grp", down)
    shared = shared + incoming[recv_slot]
    upper_face = partial_sum[:, blocks - 2] + after
    lower_face = partial_sum[:, blocks - 1] + before
    whole = jnp.concatenate(
        [
            shared.reshape(sub_here, face_count, case_count, block_width),
            upper_face[:, None],
            lower_face[:, None],
        ],
        axis=1,
    )
    return whole, landed


def apply_blocks(matrices, field):
    sub_here, blocks, case_count, block_width = field.shape
    flat = field.transpose(0, 2, 1, 3).reshape(sub_here, case_count, blocks * block_width)
    high = flat.astype(jnp.bfloat16)
    low = (flat - high.astype(jnp.float32)).astype(jnp.bfloat16)
    both = jnp.concatenate([high, low], axis=1)
    product = jnp.einsum("sri,sij->srj", both, matrices, preferred_element_type=jnp.float32)
    product = product[:, :case_count] + product[:, case_count:]
    return product.reshape(sub_here, case_count, blocks, block_width).transpose(0, 2, 1, 3)


def dot(a, b):
    return jnp.sum(a * b, axis=(0, 1, 3))


def local(
    loads, schur, local_inverse, coarse_basis, coarse_inverse, primal_index, nbr_sub, nbr_block
):
    sub_here, blocks, case_count, block_width = loads.shape
    peer_count = lax.axis_size("sub")
    device_count = peer_count * lax.axis_size("grp")
    face_count = blocks - 2
    primal_here = primal_index.size
    prim_count = coarse_inverse.shape[1]
    capacity = max(2, (sub_here * face_count + peer_count - 2) // (peer_count - 1))
    routes = face_routes(nbr_sub, nbr_block, peer_count, capacity)
    weights = (1.0 / (1.0 + (nbr_sub >= 0).astype(jnp.float32)))[:, :, None, None]

    index_row = jnp.zeros((8, block_width), jnp.float32)
    index_row = index_row.at[0, :primal_here].set(primal_index.reshape(-1).astype(jnp.float32))
    rider = jnp.broadcast_to(index_row[None], (peer_count, 8, block_width))
    resid, landed = assemble(loads, routes, rider)
    slab_index = landed[:, 0, :primal_here].astype(jnp.int32).reshape(-1)

    columns = (
        jnp.arange(prim_count, dtype=jnp.int32)[:, None] == slab_index[None, :]
    ).astype(jnp.float32)
    picked_columns = jnp.dot(coarse_inverse, columns, precision=PRECISE)
    rows_here = coarse_inverse.shape[0]
    outgoing = picked_columns.reshape(rows_here, peer_count, primal_here).transpose(1, 0, 2)
    outgoing = outgoing.reshape(peer_count, -1, block_width)

    def gather_rows(projected, extras):
        message = jnp.concatenate([projected.reshape(-1, block_width)] + extras, axis=0)
        message = jnp.broadcast_to(message[None, :, None], (device_count, message.shape[0], 1, block_width))
        return all_to_all(message, AXES)[:, :, 0]

    def project(field):
        projected = jnp.einsum("scbk,sbrk->scr", coarse_basis, field, precision=PRECISE)
        return projected.reshape(primal_here, case_count)

    message_rows = primal_here * case_count // block_width

    def spread(landed, responses):
        everyone = landed[:, :message_rows].reshape(device_count * primal_here, case_count)
        picked = lax.dot_general(
            responses, everyone, (((0,), (0,)), ((), ())), precision=PRECISE
        ).reshape(sub_here, -1, case_count)
        return jnp.einsum("scbk,scr->sbrk", coarse_basis, picked, precision=PRECISE)

    def row(*values):
        flat = jnp.concatenate(values)
        return jnp.pad(flat, (0, block_width - flat.size)).reshape(1, block_width)

    u0 = weights * resid
    landed = gather_rows(project(u0), [row(primal_index.reshape(-1).astype(jnp.float32))])
    all_index = landed[:, message_rows, :primal_here].astype(jnp.int32).reshape(-1)
    coarse_columns = all_to_all(outgoing, "sub").reshape(prim_count, primal_here)
    rows = (all_index[:, None] == jnp.arange(prim_count, dtype=jnp.int32)[None, :]).astype(
        jnp.float32
    )
    responses = jnp.dot(rows, coarse_columns, precision=PRECISE)

    c0 = apply_blocks(local_inverse, u0) + spread(landed, responses)
    dot0_here = dot(u0, c0)
    z0, _ = assemble(weights * c0, routes)
    q0 = apply_blocks(schur, z0)
    curv0_here = dot(z0, q0)
    y0, _ = assemble(q0, routes)
    v0 = weights * y0
    landed = gather_rows(project(v0), [row(dot0_here, curv0_here)])
    sums = jnp.sum(landed[:, message_rows], axis=0)
    dot0 = sums[:case_count]
    curv0 = sums[case_count : 2 * case_count]
    alpha0 = (dot0 / curv0)[None, None, :, None]
    k0 = apply_blocks(local_inverse, v0) + spread(landed, responses)
    c1 = c0 - alpha0 * k0
    u1 = u0 - alpha0 * v0
    dot1_here = dot(u1, c1)
    z1, _ = assemble(weights * c1, routes)
    q1 = apply_blocks(schur, z1)
    own_here = dot(z1, q1)
    cross_here = dot(z1, q0) + dot(z0, q1)
    y1, _ = assemble(q1, routes)
    v1 = weights * y1
    landed = gather_rows(project(v1), [row(dot1_here, own_here, cross_here)])
    sums = jnp.sum(landed[:, message_rows], axis=0)
    dot1 = sums[:case_count]
    own = sums[case_count : 2 * case_count]
    cross = sums[2 * case_count : 3 * case_count]
    ratio = dot1 / dot0
    curv1 = own + ratio * (cross + ratio * curv0)
    alpha1 = (dot1 / curv1)[None, None, :, None]
    beta = ratio[None, None, :, None]
    k1 = apply_blocks(local_inverse, v1) + spread(landed, responses)
    c2 = c1 - alpha1 * (k1 + beta * k0)
    precond, _ = assemble(weights * c2, routes)
    result = alpha0 * z0 + alpha1 * (z1 + beta * z0)
    return (result, precond)


def solution(mesh):
    in_specs = (
        P(AXES, None, None, None),
        P(AXES, None, None),
        P(AXES, None, None),
        P(AXES, None, None, None),
        P("sub", None),
        P(AXES, None),
        P(AXES, None),
        P(AXES, None),
    )
    out_specs = (P(AXES, None, None, None), P(AXES, None, None, None))
    return jax.shard_map(local, mesh=mesh, in_specs=in_specs, out_specs=out_specs, check_vma=False)
```

```python
import functools

import jax
import jax.numpy as jnp
from jax import lax
from jax.experimental import pallas as pl
from jax.experimental.pallas import tpu as pltpu
from jax.sharding import PartitionSpec as P

AXES = ("grp", "sub")
PRECISE = lax.Precision.HIGHEST
F32 = jnp.float32
BF16 = jnp.bfloat16
SMEM = pl.BlockSpec(memory_space=pltpu.SMEM)
VMEM = pl.BlockSpec(memory_space=pltpu.VMEM)
HBM = pl.BlockSpec(memory_space=pltpu.HBM)
VMEM_LIMIT = 60 * 1024 * 1024


def shape(dims, dtype=F32):
    return jax.ShapeDtypeStruct(dims, dtype)


def params():
    return pltpu.CompilerParams(vmem_limit_bytes=VMEM_LIMIT)


def cost(flops, moved):
    return pl.CostEstimate(flops=flops, bytes_accessed=moved, transcendentals=0)


def face_routes(nbr_sub, nbr_block, peer_count, capacity):
    subs, blocks = nbr_sub.shape
    face_count = blocks - 2
    shared = lax.broadcasted_iota(jnp.int32, nbr_sub.shape, 1) < face_count
    place = lax.broadcasted_iota(jnp.int32, nbr_sub.shape, 0) * face_count
    place = place + lax.broadcasted_iota(jnp.int32, nbr_sub.shape, 1)
    peer = jnp.where(shared, nbr_sub // subs % peer_count, -1)
    partner_place = nbr_sub % subs * face_count + nbr_block
    same = (peer[:, :, None, None] == peer[None, None]) & shared[None, None]

    def rank(order):
        return jnp.sum(same & (order[None, None] < order[:, :, None, None]), axis=(2, 3))

    first = jnp.maximum(peer, 0) * capacity
    return (first + rank(place), first + rank(partner_place))


def weight(nbr, s, b):
    return jnp.where(nbr[s, b] >= 0, 0.5, 1.0).astype(F32)


def split(x):
    high = x.astype(BF16)
    return high, (x - high.astype(F32)).astype(BF16)


def dotted(a, b):
    return lax.dot_general(a, b, (((1,), (0,)), ((), ())), preferred_element_type=F32)


def three_part(both, other):
    product = dotted(both, other)
    rows, columns = product.shape[0] // 2, product.shape[1] // 2
    return product[:rows, :columns] + product[:rows, columns:] + product[rows:, :columns]


def slot_of(buffer, slot, cases, capacity):
    start = pl.multiple_of(lax.rem(slot, capacity) * cases, cases)
    return buffer.at[lax.div(slot, capacity), pl.ds(start, cases)]


def sends(source, slots, capacity, outgoing, sems, s):
    faces = source.shape[1] - 2
    cases = source.shape[2]
    return [
        pltpu.make_async_copy(
            source.at[s, b], slot_of(outgoing, slots[s, b], cases, capacity), sems.at[s, b]
        )
        for b in range(faces)
    ]


def rims(source, upward, downward, sems):
    faces = source.shape[1] - 2
    return [
        pltpu.make_async_copy(source.at[:, faces], upward, sems.at[0, faces]),
        pltpu.make_async_copy(source.at[:, faces + 1], downward, sems.at[0, faces + 1]),
    ]


def fetches(landing, slots, capacity, incoming, before, after, sems):
    subs, blocks, cases = landing.shape[:3]
    faces = blocks - 2
    copies = [
        [
            pltpu.make_async_copy(
                slot_of(incoming, slots[s, b], cases, capacity), landing.at[s, b], sems.at[s, b]
            )
            for b in range(faces)
        ]
        for s in range(subs)
    ]
    copies.append(
        [
            pltpu.make_async_copy(after, landing.at[:, faces], sems.at[0, faces]),
            pltpu.make_async_copy(before, landing.at[:, faces + 1], sems.at[0, faces + 1]),
        ]
    )
    return copies


def start_all(copies):
    for copy in copies:
        copy.start()
    return copies


def wait_all(copies):
    for copy in copies:
        copy.wait()


def pack_kernel(
    capacity, slots, primal, loads, outgoing, upward, downward, index_row, tall, sems, row_sem
):
    subs, blocks, cases, width = loads.shape
    coarse = primal.shape[1]
    copies = start_all(rims(loads, upward, downward, sems))
    for s in range(subs):
        copies += start_all(sends(loads, slots, capacity, outgoing, sems, s))
    lane = lax.broadcasted_iota(jnp.int32, (1, width), 1)
    row = jnp.zeros((1, width), jnp.int32)
    for s in range(subs):
        for c in range(coarse):
            row = jnp.where(lane == s * coarse + c, primal[s, c], row)
    row = row.astype(F32)
    index_row[...] = row
    tall[...] = jnp.broadcast_to(row[None], tall.shape)
    rows = outgoing.at[:, pl.ds(capacity * cases, tall.shape[1])]
    copies += start_all([pltpu.make_async_copy(tall, rows, row_sem)])
    wait_all(copies)


def project_kernel(
    dot_count, capacity, nbr, slots, incoming, before, after, base, basis, *rest
):
    dots = rest[:dot_count]
    field, message, landing, parts, tall, sems = rest[dot_count:]
    subs, blocks, cases, width = base.shape
    lanes = subs * cases
    copies = fetches(landing, slots, capacity, incoming, before, after, sems)
    for group in copies:
        start_all(group)
    wait_all(copies[subs])
    for s in range(subs):
        wait_all(copies[s])
        for b in range(blocks):
            value = weight(nbr, s, b) * (base[s, b] + landing[s, b])
            field[s, b] = value
            high, low = split(value)
            parts[s * cases : (s + 1) * cases, b * width : (b + 1) * width] = high
            parts[lanes + s * cases : lanes + (s + 1) * cases, b * width : (b + 1) * width] = low
    primal = basis.shape[0] // 4
    product = lax.dot_general(
        basis[: 2 * primal], parts[...], (((1,), (1,)), ((), ())), preferred_element_type=F32
    )
    product = product[:primal, :lanes] + product[:primal, lanes:] + product[primal:, :lanes]
    coarse = primal // subs
    lane = lax.broadcasted_iota(jnp.int32, (coarse, lanes), 1) // cases
    block = jnp.zeros((coarse, lanes), F32)
    for s in range(subs):
        block = jnp.where(lane == s, product[s * coarse : (s + 1) * coarse], block)
    if dots[0].shape[0] == 1:
        row = dots[0][...]
    else:
        tall[...] = jnp.zeros_like(tall)
        place = 0
        for part in dots:
            tall[place : place + part.shape[0]] = part[...]
            place += part.shape[0]
        row = jnp.sum(tall[...].T, axis=0, keepdims=True)
    period = coarse + 1
    for p in range(message.shape[0] // period):
        message[p * period : p * period + coarse] = block
        message[p * period + coarse : (p + 1) * period] = row


def applied(flat, matrix, fine):
    if not fine:
        return dotted(flat.astype(BF16), matrix)
    both = dotted(jnp.concatenate(split(flat), axis=0), matrix)
    return both[: flat.shape[0]] + both[flat.shape[0] :]


def inverse_kernel(fine, field, matrix, out, held, sems):
    subs, blocks, cases, width = field.shape
    copies = start_all(
        [pltpu.make_async_copy(matrix.at[s], held.at[s], sems.at[s]) for s in range(subs)]
    )
    for s in range(subs):
        flat = jnp.concatenate([field[s, b] for b in range(blocks)], axis=1)
        copies[s].wait()
        product = applied(flat, held[s], fine)
        for b in range(blocks):
            out[s, b] = product[:, b * width : (b + 1) * width]


def folded(product, primal):
    size = product.shape[0]
    turned = product.T
    row = lax.broadcasted_iota(jnp.int32, (size, size), 0) // primal
    lane = lax.broadcasted_iota(jnp.int32, (size, size), 1) // primal
    kept = jnp.where(row == lane, turned, 0.0)
    total = kept[:primal]
    for q in range(1, size // primal):
        total = total + kept[q * primal : (q + 1) * primal]
    out = total
    for q in range(1, size // primal):
        out = out + pltpu.roll(total, q * primal, 1)
    return out


def spread(picked, basis, subs, coarse):
    cases, lanes = picked.shape
    high = picked.astype(BF16).astype(F32)
    lane = lax.broadcasted_iota(jnp.int32, (cases, lanes), 1)
    parts = jnp.where(lane < lanes // 2, high, picked - high)
    owner = lane // coarse % subs
    tall = jnp.concatenate(
        [jnp.where(owner == s, parts, 0.0) for s in range(subs)], axis=0
    ).astype(BF16)
    return dotted(tall, basis[...])


def first_kernel(
    capacity, nbr, slots, columns, totals, basis, local_part, field,
    corrected, dots, outgoing, upward, downward, weighted, sems,
):
    subs, blocks, cases, width = field.shape
    primal = basis.shape[0] // 4
    high, low = split(columns[...].T)
    total_high, total_low = split(totals[...])
    product = three_part(
        jnp.concatenate([high, low], axis=0), jnp.concatenate([total_high, total_low], axis=1)
    )
    coarse_part = spread(folded(product, primal), basis, subs, primal // subs)
    dot = jnp.zeros((cases, width), F32)
    copies = []
    for s in range(subs):
        for b in range(blocks):
            value = local_part[s, b] + coarse_part[
                s * cases : (s + 1) * cases, b * width : (b + 1) * width
            ]
            corrected[s, b] = value
            weighted[s, b] = weight(nbr, s, b) * value
            dot = dot + field[s, b] * value
        copies += start_all(sends(weighted, slots, capacity, outgoing, sems, s))
    copies += start_all(rims(weighted, upward, downward, sems))
    dots[...] = dot
    wait_all(copies)


def everyone(landed, period):
    value = landed[...]
    row = lax.broadcasted_iota(jnp.int32, value.shape, 0)
    sums = lax.rem(row, period) == period - 1
    totals = jnp.sum(jnp.where(sums, value, 0.0), axis=0, keepdims=True)
    totals = jnp.broadcast_to(totals, (value.shape[1], value.shape[1])).T
    high, low = split(jnp.where(sums, 0.0, value))
    return totals, jnp.concatenate([high, low], axis=1)


def second_kernel(
    capacity, nbr, slots, landed, responses, basis, local_part, corrected, field, image,
    direction_part, out, dots, scalars, outgoing, upward, downward, weighted, sems,
):
    subs, blocks, cases, width = field.shape
    primal = basis.shape[0] // 4
    coarse = primal // subs
    totals, rows = everyone(landed, coarse + 1)
    dot0 = totals[:cases]
    curv0 = totals[cases : 2 * cases]
    alpha = dot0 / curv0
    scalars[0] = dot0
    scalars[1] = curv0
    scalars[2] = alpha
    product = three_part(responses[...], rows)
    coarse_part = spread(folded(product, primal), basis, subs, coarse)
    dot = jnp.zeros((cases, width), F32)
    copies = []
    for s in range(subs):
        for b in range(blocks):
            step = local_part[s, b] + coarse_part[
                s * cases : (s + 1) * cases, b * width : (b + 1) * width
            ]
            direction_part[s, b] = step
            value = corrected[s, b] - alpha * step
            out[s, b] = value
            weighted[s, b] = weight(nbr, s, b) * value
            dot = dot + (field[s, b] - alpha * image[s, b]) * value
        copies += start_all(sends(weighted, slots, capacity, outgoing, sems, s))
    copies += start_all(rims(weighted, upward, downward, sems))
    dots[...] = dot
    wait_all(copies)


def third_kernel(
    capacity, nbr, slots, landed, responses, basis, local_part, direction_part, corrected, scalars,
    weighted, factors, outgoing, upward, downward, sems,
):
    subs, blocks, cases, width = corrected.shape
    primal = basis.shape[0] // 4
    coarse = primal // subs
    totals, rows = everyone(landed, coarse + 1)
    dot1 = totals[:cases]
    own = totals[cases : 2 * cases]
    cross = totals[2 * cases : 3 * cases]
    beta = dot1 / scalars[0]
    curv1 = own + beta * (cross + beta * scalars[1])
    alpha = dot1 / curv1
    factors[0] = scalars[2] + alpha * beta
    factors[1] = alpha
    product = three_part(responses[...], rows)
    coarse_part = spread(folded(product, primal), basis, subs, coarse)
    copies = []
    for s in range(subs):
        for b in range(blocks):
            step = local_part[s, b] + coarse_part[
                s * cases : (s + 1) * cases, b * width : (b + 1) * width
            ]
            value = corrected[s, b] - alpha * (step + beta * direction_part[s, b])
            weighted[s, b] = weight(nbr, s, b) * value
        copies += start_all(sends(weighted, slots, capacity, outgoing, sems, s))
    copies += start_all(rims(weighted, upward, downward, sems))
    wait_all(copies)


def schur_kernel(
    older, capacity, nbr, send_slots, recv_slots, incoming, before, after, matrix, corrected, *rest
):
    if older:
        old_direction, old_product = rest[:2]
        rest = rest[2:]
    direction, product, dots, outgoing, upward, downward, landing, held, sems, held_sems = rest
    subs, blocks, cases, width = corrected.shape
    copies = fetches(landing, recv_slots, capacity, incoming, before, after, sems)
    loads = [pltpu.make_async_copy(matrix.at[s], held.at[s], held_sems.at[s]) for s in range(subs)]
    loads[0].start()
    for group in copies:
        start_all(group)
    start_all(loads[1:])
    wait_all(copies[subs])
    own = jnp.zeros((cases, width), F32)
    cross = jnp.zeros((cases, width), F32)
    out = []
    for s in range(subs):
        wait_all(copies[s])
        flat = []
        for b in range(blocks):
            value = weight(nbr, s, b) * corrected[s, b] + landing[s, b]
            direction[s, b] = value
            flat.append(value)
        flat = jnp.concatenate(flat, axis=1)
        loads[s].wait()
        both = applied(flat, held[s], older)
        for b in range(blocks):
            piece = both[:, b * width : (b + 1) * width]
            product[s, b] = piece
            own = own + direction[s, b] * piece
            if older:
                cross = cross + direction[s, b] * old_product[s, b] + old_direction[s, b] * piece
        out += start_all(sends(product, send_slots, capacity, outgoing, sems, s))
    out += start_all(rims(product, upward, downward, sems))
    dots[0:cases] = own
    if older:
        dots[cases:] = cross
    wait_all(out)


def last_kernel(capacity, slots, incoming, before, after, base, out, landing, sems):
    subs, blocks = base.shape[:2]
    copies = fetches(landing, slots, capacity, incoming, before, after, sems)
    for group in copies:
        start_all(group)
    wait_all(copies[subs])
    for s in range(subs):
        wait_all(copies[s])
        for b in range(blocks):
            out[s, b] = base[s, b] + landing[s, b]


def row_numbers(shape, rows_here, groups):
    row = lax.broadcasted_iota(jnp.int32, shape, 0)
    quarter = rows_here // groups
    return row // quarter * rows_here + row % quarter


def totals_kernel(rows_here, index_period, landed, index, totals):
    groups = index.shape[0]
    lanes = landed.shape[1]
    cases = lanes // groups
    period = index_period
    value = landed[...]
    row = lax.broadcasted_iota(jnp.int32, value.shape, 0)
    high, low = split(jnp.where(lax.rem(row, period) == period - 1, 0.0, value))
    rows = jnp.concatenate([high, low], axis=1)
    height = totals.shape[0]
    number = row_numbers((height, landed.shape[0]), rows_here, groups)
    lane = lax.broadcasted_iota(jnp.int32, (height, lanes), 1) // cases
    out = jnp.zeros((height, lanes), F32)
    for a in range(groups):
        gathered = jnp.zeros((height, lanes), F32)
        for q in range(groups):
            chosen = number == index[q : q + 1, :] - a * (rows_here // groups)
            product = dotted(jnp.where(chosen, 1.0, 0.0).astype(BF16), rows)
            gathered = jnp.where(lane == q, product[:, :lanes] + product[:, lanes:], gathered)
        summed = gathered
        for q in range(1, groups):
            summed = summed + pltpu.roll(gathered, q * cases, 1)
        out = jnp.where(lane == a, summed, out)
    totals[...] = out


def responses_kernel(rows_here, columns, index, responses):
    groups = index.shape[0]
    lanes = columns.shape[1]
    primal = lanes // groups
    high, low = split(columns[...].T)
    number = row_numbers((columns.shape[0], index.shape[1]), rows_here, groups)
    for q in range(groups):
        total = jnp.zeros((2 * primal, index.shape[1]), F32)
        for a in range(groups):
            chosen = number == index[q : q + 1, :] - a * (rows_here // groups)
            both = jnp.concatenate(
                [high[a * primal : (a + 1) * primal], low[a * primal : (a + 1) * primal]], axis=0
            )
            total = total + dotted(both, jnp.where(chosen, 1.0, 0.0).astype(BF16))
        responses[q * primal : (q + 1) * primal] = total[:primal].astype(BF16)
        responses[lanes + q * primal : lanes + (q + 1) * primal] = total[primal:].astype(BF16)


def all_to_all(block, axes):
    return lax.all_to_all(block, axes, split_axis=0, concat_axis=0, tiled=True)


def local(
    loads, schur, local_inverse, coarse_basis, coarse_inverse, primal_index, nbr_sub, nbr_block
):
    subs, blocks, cases, width = loads.shape
    coarse = primal_index.shape[1]
    primal = subs * coarse
    groups = subs
    faces = blocks - 2
    peers = lax.axis_size("sub")
    slabs = lax.axis_size("grp")
    devices = peers * slabs
    rows_here, prim_count = coarse_inverse.shape
    capacity = max(2, (subs * faces + peers - 2) // (peers - 1))
    period = coarse + 1
    size = blocks * width
    field_shape = loads.shape
    rim = (subs, cases, width)
    slot_shape = (peers, capacity * cases, width)
    face_sems = pltpu.SemaphoreType.DMA((subs, blocks))
    held_scratch = [pltpu.VMEM((subs, size, size), BF16), pltpu.SemaphoreType.DMA((subs,))]
    field_bytes = 4 * subs * blocks * cases * width
    matrix_bytes = 2 * subs * size * size
    matrix_flops = 4 * subs * cases * size * size

    send_slots, recv_slots = face_routes(nbr_sub, nbr_block, peers, capacity)
    up = [(i, i + 1) for i in range(slabs - 1)]
    down = [(j, i) for i, j in up]

    def exchange(outgoing, upward, downward):
        incoming = all_to_all(outgoing, "sub")
        before = lax.ppermute(upward, "grp", up)
        after = lax.ppermute(downward, "grp", down)
        return incoming, before, after

    def gather_rows(message):
        message = message.reshape(devices, period, 1, width)
        return all_to_all(message, AXES).reshape(devices * period, width)

    *packed, index_row = pl.pallas_call(
        functools.partial(pack_kernel, capacity),
        out_shape=(
            shape((peers, capacity * cases + 8, width)), shape(rim), shape(rim),
            shape((1, width)),
        ),
        in_specs=[SMEM, SMEM, VMEM],
        out_specs=(HBM, HBM, HBM, VMEM),
        scratch_shapes=[
            pltpu.VMEM((peers, 8, width), F32), face_sems, pltpu.SemaphoreType.DMA(())
        ],
        compiler_params=params(),
        cost_estimate=cost(0, 2 * field_bytes),
        name="pack",
    )(send_slots, primal_index, loads)
    incoming, before, after = exchange(*packed)
    slab_index = incoming[:, capacity * cases, :primal].astype(jnp.int32).reshape(-1)

    flat_basis = coarse_basis.reshape(primal, size)
    basis_high = lax.reduce_precision(flat_basis, 8, 7)
    basis_low = flat_basis - basis_high
    basis = jnp.concatenate([basis_high, basis_low, basis_high, basis_low], axis=0).astype(BF16)

    def project(incoming, base, before, after, dots):
        return pl.pallas_call(
            functools.partial(project_kernel, len(dots), capacity),
            out_shape=(shape(field_shape), shape((devices * period, width))),
            in_specs=[SMEM, SMEM] + [HBM] * 3 + [VMEM] * (2 + len(dots)),
            out_specs=(VMEM, VMEM),
            scratch_shapes=[
                pltpu.VMEM(field_shape, F32),
                pltpu.VMEM((2 * subs * cases, size), BF16),
                pltpu.VMEM((width, width), F32),
                face_sems,
            ],
            compiler_params=params(),
            cost_estimate=cost(8 * primal * subs * cases * size, 5 * field_bytes),
            name="project",
        )(nbr_sub, recv_slots, incoming, before, after, base, basis, *dots)

    def inverse(field, fine):
        return pl.pallas_call(
            functools.partial(inverse_kernel, fine),
            out_shape=shape(field_shape),
            in_specs=[VMEM, HBM],
            out_specs=VMEM,
            scratch_shapes=held_scratch,
            compiler_params=params(),
            cost_estimate=cost(matrix_flops, matrix_bytes + 2 * field_bytes),
            name="inverse",
        )(field, local_inverse)

    def apply_schur(incoming, corrected, before, after, old=()):
        count = 2 if old else 1
        return pl.pallas_call(
            functools.partial(schur_kernel, bool(old), capacity),
            out_shape=(
                shape(field_shape), shape(field_shape), shape((count * cases, width)),
                shape(slot_shape), shape(rim), shape(rim),
            ),
            in_specs=[SMEM] * 3 + [HBM] * 4 + [VMEM] * (1 + len(old)),
            out_specs=(VMEM, VMEM, VMEM, HBM, HBM, HBM),
            scratch_shapes=[
                pltpu.VMEM(field_shape, F32), held_scratch[0], face_sems, held_scratch[1]
            ],
            compiler_params=params(),
            cost_estimate=cost(matrix_flops, matrix_bytes + 6 * field_bytes),
            name="schur",
        )(nbr_sub, send_slots, recv_slots, incoming, before, after, schur, corrected, *old)

    sent_shapes = (shape(slot_shape), shape(rim), shape(rim))
    sent_specs = (HBM, HBM, HBM)
    combine_cost = cost(2 * primal * 8 * 128 * size, 8 * field_bytes)

    u0, message = project(incoming, loads, before, after, (index_row,))
    landed = gather_rows(message)

    columns_at = (
        jnp.arange(prim_count, dtype=jnp.int32)[:, None] == slab_index[None, :]
    ).astype(F32)
    asked = jnp.dot(coarse_inverse, columns_at, precision=PRECISE)
    asked = asked.reshape(groups, rows_here // groups, peers, primal).transpose(2, 1, 0, 3)
    asked = asked.reshape(peers, rows_here // groups, groups * primal)
    local0 = inverse(u0, False)
    asked, landed, local0 = lax.optimization_barrier((asked, landed, local0))
    columns = all_to_all(asked, "sub").reshape(-1, groups * primal)

    index = landed.reshape(devices, period, width)[:, coarse, :primal].astype(jnp.int32)
    index = index.reshape(devices, subs, coarse).transpose(1, 0, 2)
    index = jnp.pad(index, ((0, 0), (0, 0), (0, 1)), constant_values=-prim_count)
    index = index.reshape(subs, devices * period)
    height = prim_count // groups
    totals = pl.pallas_call(
        functools.partial(totals_kernel, rows_here, period),
        out_shape=shape((height, width)),
        in_specs=[VMEM, VMEM],
        out_specs=VMEM,
        compiler_params=params(),
        cost_estimate=cost(4 * prim_count * devices * period * groups * width, 2 * field_bytes),
        name="totals",
    )(landed, index)

    c0, dot0_part, *packed = pl.pallas_call(
        functools.partial(first_kernel, capacity),
        out_shape=(shape(field_shape), shape((cases, width))) + sent_shapes,
        in_specs=[SMEM, SMEM] + [VMEM] * 5,
        out_specs=(VMEM, VMEM) + sent_specs,
        scratch_shapes=[pltpu.VMEM(field_shape, F32), face_sems],
        compiler_params=params(),
        cost_estimate=combine_cost,
        name="first",
    )(nbr_sub, send_slots, columns, totals, basis, local0, u0)
    incoming, before, after = exchange(*packed)
    responses = pl.pallas_call(
        functools.partial(responses_kernel, rows_here),
        out_shape=shape((2 * groups * primal, devices * period), BF16),
        in_specs=[VMEM, VMEM],
        out_specs=VMEM,
        compiler_params=params(),
        cost_estimate=cost(4 * primal * prim_count * devices * period * groups, field_bytes),
        name="responses",
    )(columns, index)
    z0, q0, curv0_part, *packed = apply_schur(incoming, c0, before, after)
    incoming, before, after = exchange(*packed)

    v0, message = project(incoming, q0, before, after, (dot0_part, curv0_part))
    landed = gather_rows(message)
    local1 = inverse(v0, True)
    k0, c1, dot1_part, scalars, *packed = pl.pallas_call(
        functools.partial(second_kernel, capacity),
        out_shape=(
            shape(field_shape), shape(field_shape), shape((cases, width)),
            shape((3, cases, width)),
        )
        + sent_shapes,
        in_specs=[SMEM, SMEM] + [VMEM] * 7,
        out_specs=(VMEM,) * 4 + sent_specs,
        scratch_shapes=[pltpu.VMEM(field_shape, F32), face_sems],
        compiler_params=params(),
        cost_estimate=combine_cost,
        name="second",
    )(nbr_sub, send_slots, landed, responses, basis, local1, c0, u0, v0)
    incoming, before, after = exchange(*packed)
    z1, q1, curv1_parts, *packed = apply_schur(
        incoming, c1, before, after, (z0, q0)
    )
    incoming, before, after = exchange(*packed)

    v1, message = project(incoming, q1, before, after, (dot1_part, curv1_parts))
    landed = gather_rows(message)
    local2 = inverse(v1, True)
    weighted, factors, *packed = pl.pallas_call(
        functools.partial(third_kernel, capacity),
        out_shape=(shape(field_shape), shape((2, cases, width))) + sent_shapes,
        in_specs=[SMEM, SMEM] + [VMEM] * 7,
        out_specs=(VMEM, VMEM) + sent_specs,
        scratch_shapes=[face_sems],
        compiler_params=params(),
        cost_estimate=combine_cost,
        name="third",
    )(nbr_sub, send_slots, landed, responses, basis, local2, k0, c1, scalars)
    incoming, before, after = exchange(*packed)
    result = factors[0] * z0 + factors[1] * z1
    precond = pl.pallas_call(
        functools.partial(last_kernel, capacity),
        out_shape=shape(field_shape),
        in_specs=[SMEM] + [HBM] * 3 + [VMEM],
        out_specs=VMEM,
        scratch_shapes=[pltpu.VMEM(field_shape, F32), face_sems],
        compiler_params=params(),
        cost_estimate=cost(0, 4 * field_bytes),
        name="last",
    )(recv_slots, incoming, before, after, weighted)
    return (result, precond)


def solution(mesh):
    in_specs = (
        P(AXES, None, None, None),
        P(AXES, None, None),
        P(AXES, None, None),
        P(AXES, None, None, None),
        P("sub", None),
        P(AXES, None),
        P(AXES, None),
        P(AXES, None),
    )
    out_specs = (P(AXES, None, None, None), P(AXES, None, None, None))
    return jax.shard_map(local, mesh=mesh, in_specs=in_specs, out_specs=out_specs, check_vma=False)
```

```python
import functools

import jax
import jax.numpy as jnp
from jax import lax
from jax.experimental import pallas as pl
from jax.experimental.pallas import tpu as pltpu
from jax.sharding import PartitionSpec as P

AXES = ("grp", "sub")
PRECISE = lax.Precision.HIGHEST
F32 = jnp.float32
BF16 = jnp.bfloat16
SMEM = pl.BlockSpec(memory_space=pltpu.SMEM)
VMEM = pl.BlockSpec(memory_space=pltpu.VMEM)
HBM = pl.BlockSpec(memory_space=pltpu.HBM)
VMEM_LIMIT = 63 * 1024 * 1024
PIECES = 1
FACES = 6


def shape(dims, dtype=F32):
    return jax.ShapeDtypeStruct(dims, dtype)


def params(limit=VMEM_LIMIT):
    return pltpu.CompilerParams(vmem_limit_bytes=limit)


def cost(flops, moved):
    return pl.CostEstimate(flops=flops, bytes_accessed=moved, transcendentals=0)


def face_routes(nbr_sub, nbr_block, peer_count, capacity):
    subs, blocks = nbr_sub.shape
    face_count = blocks - 2
    shared = lax.broadcasted_iota(jnp.int32, nbr_sub.shape, 1) < face_count
    place = lax.broadcasted_iota(jnp.int32, nbr_sub.shape, 0) * face_count
    place = place + lax.broadcasted_iota(jnp.int32, nbr_sub.shape, 1)
    peer = jnp.where(shared, nbr_sub // subs % peer_count, -1)
    partner_place = nbr_sub % subs * face_count + nbr_block
    same = (peer[:, :, None, None] == peer[None, None]) & shared[None, None]

    def rank(order):
        return jnp.sum(same & (order[None, None] < order[:, :, None, None]), axis=(2, 3))

    first = jnp.maximum(peer, 0) * capacity
    return (first + rank(place), first + rank(partner_place))


def weight(table, s, b):
    return jnp.where(table[s, b] >= 0, 0.5, 1.0).astype(F32)


def split(x):
    high = x.astype(BF16)
    return high, (x - high.astype(F32)).astype(BF16)


def dotted(a, b):
    return lax.dot_general(a, b, (((1,), (0,)), ((), ())), preferred_element_type=F32)


def three_part(both, other):
    product = dotted(both, other)
    rows, columns = product.shape[0] // 2, product.shape[1] // 2
    return product[:rows, :columns] + product[:rows, columns:] + product[rows:, :columns]


def slot_of(buffer, slot, cases):
    capacity = buffer.shape[1] // cases
    start = pl.multiple_of(lax.rem(slot, capacity) * cases, cases)
    return buffer.at[lax.div(slot, capacity), pl.ds(start, cases)]


def sends(source, table, outgoing, sems, s):
    subs, blocks, cases = source.shape[:3]
    return [
        pltpu.make_async_copy(
            source.at[s, b], slot_of(outgoing, table[subs + s, b], cases), sems.at[s, b]
        )
        for b in range(blocks - 2)
    ]


def rims(source, upward, downward, sems):
    faces = source.shape[1] - 2
    return [
        pltpu.make_async_copy(source.at[:, faces], upward, sems.at[0, faces]),
        pltpu.make_async_copy(source.at[:, faces + 1], downward, sems.at[0, faces + 1]),
    ]


def fetches(table, table_s, incoming, incoming_v, before, after, rims_v, sems):
    return start_all(
        copies_of(
            [table, incoming, after, before],
            [table_s, incoming_v, rims_v.at[0], rims_v.at[1]], sems, 0,
        )
    )


def received(table_s, incoming_v, rims_v, s, b):
    subs, cases = rims_v.shape[1:3]
    faces = FACES
    if b >= faces:
        return rims_v[b - faces, s]
    slot = table_s[2 * subs + s, b]
    capacity = incoming_v.shape[1] // cases
    start = pl.multiple_of(lax.rem(slot, capacity) * cases, cases)
    return incoming_v[lax.div(slot, capacity), pl.ds(start, cases)]


def start_all(copies):
    for copy in copies:
        copy.start()
    return copies


def wait_all(copies):
    for copy in copies:
        copy.wait()


def copies_of(sources, targets, sems, first):
    return [
        pltpu.make_async_copy(source, target, sems.at[first + i])
        for i, (source, target) in enumerate(zip(sources, targets))
    ]


def parts_of(ref):
    return [ref.at[s] for s in range(ref.shape[0])]


def pack_kernel(
    table, primal, loads, outgoing, upward, downward, index_row, tall, sems, row_sem
):
    subs, blocks, cases, width = loads.shape
    coarse = primal.shape[1]
    copies = start_all(rims(loads, upward, downward, sems))
    for s in range(subs):
        copies += start_all(sends(loads, table, outgoing, sems, s))
    lane = lax.broadcasted_iota(jnp.int32, (1, width), 1)
    row = jnp.zeros((1, width), jnp.int32)
    for s in range(subs):
        for c in range(coarse):
            row = jnp.where(lane == s * coarse + c, primal[s, c], row)
    row = row.astype(F32)
    index_row[...] = jnp.broadcast_to(row, index_row.shape)
    tall[...] = jnp.broadcast_to(row[None], tall.shape)
    rows = outgoing.at[:, pl.ds(outgoing.shape[1] - tall.shape[1], tall.shape[1])]
    copies += start_all([pltpu.make_async_copy(tall, rows, row_sem)])
    wait_all(copies)


def project_kernel(
    dot_count, table, incoming, before, after, base, basis, *rest
):
    dots = rest[:dot_count]
    field, message, held, parts, factors, tall, block_rows = rest[dot_count : dot_count + 7]
    table_s, incoming_v, rims_v, sems, more = rest[dot_count + 7 :]
    subs, blocks, cases, width = base.shape
    lanes = subs * cases
    primal = basis.shape[0] // 4
    coarse = primal // subs
    arriving = fetches(table, table_s, incoming, incoming_v, before, after, rims_v, sems)
    base_in = start_all(copies_of(parts_of(base), parts_of(held), more, 0))
    others = [basis.at[pl.ds(0, 2 * primal)]]
    targets = [factors]
    place = 0
    for part in dots:
        others.append(part)
        targets.append(tall.at[pl.ds(place, part.shape[0])])
        place += part.shape[0]
    others = start_all(copies_of(others, targets, more, subs))
    tall[place:] = jnp.zeros((tall.shape[0] - place, width), F32)
    wait_all(arriving)
    out = []
    for s in range(subs):
        wait_all(base_in[s : s + 1])
        for b in range(blocks):
            other = received(table_s, incoming_v, rims_v, s, b)
            value = weight(table_s, s, b) * (held[s, b] + other)
            held[s, b] = value
            high, low = split(value)
            parts[s * cases : (s + 1) * cases, b * width : (b + 1) * width] = high
            parts[lanes + s * cases : lanes + (s + 1) * cases, b * width : (b + 1) * width] = low
        out += start_all(copies_of([held.at[s]], [field.at[s]], more, 8 + s))
    wait_all(others)
    product = lax.dot_general(
        factors[...], parts[...], (((1,), (1,)), ((), ())), preferred_element_type=F32
    )
    product = product[:primal, :lanes] + product[:primal, lanes:] + product[primal:, :lanes]
    lane = lax.broadcasted_iota(jnp.int32, (coarse, lanes), 1) // cases
    block = jnp.zeros((coarse, lanes), F32)
    for s in range(subs):
        block = jnp.where(lane == s, product[s * coarse : (s + 1) * coarse], block)
    if dot_count == 1:
        row = tall[0:1]
    else:
        row = jnp.sum(tall[...].T, axis=0, keepdims=True)
    period = coarse + 1
    height = block_rows.shape[0]
    for p in range(height // period):
        block_rows[p * period : p * period + coarse] = block
        block_rows[p * period + coarse : (p + 1) * period] = row
    count = message.shape[0] // height
    rows = [message.at[pl.ds(i * height, height)] for i in range(count)]
    out += start_all(copies_of([block_rows] * count, rows, more, 8 + subs))
    wait_all(out)


def applied(flat, matrix, fine):
    if not fine:
        return dotted(flat.astype(BF16), matrix)
    both = dotted(jnp.concatenate(split(flat), axis=0), matrix)
    return both[: flat.shape[0]] + both[flat.shape[0] :]


def pieces(matrix, held, sems):
    subs, rows = matrix.shape[:2]
    count = sems.shape[1]
    height = rows // count
    return [
        [
            pltpu.make_async_copy(
                matrix.at[s, pl.ds(i * height, height)],
                held.at[s, pl.ds(i * height, height)],
                sems.at[s, i],
            )
            for i in range(count)
        ]
        for s in range(subs)
    ]


def inverse_kernel(fine, field, matrix, out, held, sems):
    subs, blocks, cases, width = field.shape
    copies = [start_all(group) for group in pieces(matrix, held, sems)]
    for s in range(subs):
        flat = jnp.concatenate([field[s, b] for b in range(blocks)], axis=1)
        wait_all(copies[s])
        product = applied(flat, held[s], fine)
        for b in range(blocks):
            out[s, b] = product[:, b * width : (b + 1) * width]


def folded(product, primal):
    size = product.shape[0]
    turned = product.T
    row = lax.broadcasted_iota(jnp.int32, (size, size), 0) // primal
    lane = lax.broadcasted_iota(jnp.int32, (size, size), 1) // primal
    kept = jnp.where(row == lane, turned, 0.0)
    total = kept[:primal]
    for q in range(1, size // primal):
        total = total + kept[q * primal : (q + 1) * primal]
    out = total
    for q in range(1, size // primal):
        out = out + pltpu.roll(total, q * primal, 1)
    return out


def spread(picked, basis, subs, coarse):
    cases, lanes = picked.shape
    high = picked.astype(BF16).astype(F32)
    lane = lax.broadcasted_iota(jnp.int32, (cases, lanes), 1)
    parts = jnp.where(lane < lanes // 2, high, picked - high)
    owner = lane // coarse % subs
    tall = jnp.concatenate(
        [jnp.where(owner == s, parts, 0.0) for s in range(subs)], axis=0
    ).astype(BF16)
    return dotted(tall, basis[...])


def first_kernel(
    table, columns, totals, basis, local_part,
    corrected, outgoing, upward, downward,
    columns_v, totals_v, basis_v, local_v, weighted, table_s, sems, more,
):
    subs, blocks, cases, width = local_part.shape
    primal = basis.shape[0] // 4
    routes = start_all([pltpu.make_async_copy(table, table_s, sems.at[0, 0])])
    small = start_all(
        copies_of([columns, totals, basis], [columns_v, totals_v, basis_v], more, 0)
    )
    local_in = start_all(copies_of(parts_of(local_part), parts_of(local_v), more, 3))
    wait_all(small)
    wait_all(routes)
    high, low = split(columns_v[...].T)
    total_high, total_low = split(totals_v[...])
    product = three_part(
        jnp.concatenate([high, low], axis=0), jnp.concatenate([total_high, total_low], axis=1)
    )
    coarse_part = spread(folded(product, primal), basis_v, subs, primal // subs)
    out = []
    for s in range(subs):
        wait_all([local_in[s]])
        for b in range(blocks):
            value = local_v[s, b] + coarse_part[
                s * cases : (s + 1) * cases, b * width : (b + 1) * width
            ]
            local_v[s, b] = value
            weighted[s, b] = weight(table_s, s, b) * value
        out += start_all(sends(weighted, table_s, outgoing, sems, s))
        out += start_all(copies_of([local_v.at[s]], [corrected.at[s]], more, 3 + 2 * subs + s))
    out += start_all(rims(weighted, upward, downward, sems))
    wait_all(out)


def everyone(value, period):
    row = lax.broadcasted_iota(jnp.int32, value.shape, 0)
    sums = lax.rem(row, period) == period - 1
    totals = jnp.sum(jnp.where(sums, value, 0.0), axis=0, keepdims=True)
    totals = jnp.broadcast_to(totals, (value.shape[1], value.shape[1])).T
    high, low = split(jnp.where(sums, 0.0, value))
    return totals, jnp.concatenate([high, low], axis=1)


def second_kernel(
    table, landed, responses, basis, local_part, corrected,
    step_out, out_field, scalars, outgoing, upward, downward,
    landed_v, responses_v, basis_v, local_v, corrected_v, weighted, scalars_v, table_s, sems, more,
):
    subs, blocks, cases, width = corrected.shape
    primal = basis.shape[0] // 4
    coarse = primal // subs
    routes = start_all([pltpu.make_async_copy(table, table_s, sems.at[0, 0])])
    small = start_all(
        copies_of([landed, responses, basis], [landed_v, responses_v, basis_v], more, 0)
    )
    fields = [
        start_all(copies_of(parts_of(source), parts_of(target), more, 3 + i * subs))
        for i, (source, target) in enumerate(
            [(local_part, local_v), (corrected, corrected_v)]
        )
    ]
    wait_all(small)
    wait_all(routes)
    totals, rows = everyone(landed_v[...], coarse + 1)
    dot0 = totals[:cases]
    curv0 = totals[cases : 2 * cases]
    alpha = dot0 / curv0
    scalars_v[0] = dot0
    scalars_v[1] = curv0
    scalars_v[2] = alpha
    out = start_all(copies_of([scalars_v], [scalars], more, 3 + 6 * subs))
    product = three_part(responses_v[...], rows)
    coarse_part = spread(folded(product, primal), basis_v, subs, coarse)
    for s in range(subs):
        wait_all([group[s] for group in fields])
        for b in range(blocks):
            step = local_v[s, b] + coarse_part[
                s * cases : (s + 1) * cases, b * width : (b + 1) * width
            ]
            local_v[s, b] = step
            value = corrected_v[s, b] - alpha * step
            corrected_v[s, b] = value
            weighted[s, b] = weight(table_s, s, b) * value
        out += start_all(sends(weighted, table_s, outgoing, sems, s))
        out += start_all(
            copies_of(
                [local_v.at[s], corrected_v.at[s]], [step_out.at[s], out_field.at[s]],
                more, 3 + 4 * subs + 2 * s,
            )
        )
    out += start_all(rims(weighted, upward, downward, sems))
    wait_all(out)


def third_kernel(
    table, landed, responses, basis, local_part, older_step, corrected, scalars,
    weighted_out, factors, outgoing, upward, downward,
    landed_v, responses_v, basis_v, scalars_v, local_v, older_v, corrected_v, weighted,
    factors_v, table_s, sems, more,
):
    subs, blocks, cases, width = corrected.shape
    primal = basis.shape[0] // 4
    coarse = primal // subs
    routes = start_all([pltpu.make_async_copy(table, table_s, sems.at[0, 0])])
    small = start_all(
        copies_of(
            [landed, responses, basis, scalars],
            [landed_v, responses_v, basis_v, scalars_v], more, 0,
        )
    )
    fields = [
        start_all(copies_of(parts_of(source), parts_of(target), more, 4 + i * subs))
        for i, (source, target) in enumerate(
            [(local_part, local_v), (older_step, older_v), (corrected, corrected_v)]
        )
    ]
    wait_all(small)
    wait_all(routes)
    totals, rows = everyone(landed_v[...], coarse + 1)
    dot1 = totals[:cases]
    own = totals[cases : 2 * cases]
    cross = totals[2 * cases : 3 * cases]
    beta = dot1 / scalars_v[0]
    curv1 = own + beta * (cross + beta * scalars_v[1])
    alpha = dot1 / curv1
    factors_v[0] = scalars_v[2] + alpha * beta
    factors_v[1] = alpha
    out = start_all(copies_of([factors_v], [factors], more, 4 + 3 * subs))
    product = three_part(responses_v[...], rows)
    coarse_part = spread(folded(product, primal), basis_v, subs, coarse)
    for s in range(subs):
        wait_all([group[s] for group in fields])
        for b in range(blocks):
            step = local_v[s, b] + coarse_part[
                s * cases : (s + 1) * cases, b * width : (b + 1) * width
            ]
            value = corrected_v[s, b] - alpha * (step + beta * older_v[s, b])
            weighted[s, b] = weight(table_s, s, b) * value
        out += start_all(sends(weighted, table_s, outgoing, sems, s))
        out += start_all(
            copies_of([weighted.at[s]], [weighted_out.at[s]], more, 5 + 3 * subs + s)
        )
    out += start_all(rims(weighted, upward, downward, sems))
    wait_all(out)


def schur_kernel(
    fine, table, incoming, before, after, corrected, matrix,
    direction, product, outgoing, upward, downward,
    corrected_v, product_v, held, held_sems, table_s, incoming_v, rims_v, arrive_sems, sems, more,
):
    subs, blocks, cases, width = corrected.shape
    arriving = fetches(table, table_s, incoming, incoming_v, before, after, rims_v, arrive_sems)
    base_in = start_all(copies_of(parts_of(corrected), parts_of(corrected_v), more, 0))
    matrix_in = [start_all(group) for group in pieces(matrix, held, held_sems)]
    wait_all(arriving)
    out = []
    for s in range(subs):
        wait_all(base_in[s : s + 1])
        flat = []
        for b in range(blocks):
            other = received(table_s, incoming_v, rims_v, s, b)
            value = weight(table_s, s, b) * corrected_v[s, b] + other
            corrected_v[s, b] = value
            flat.append(value)
        out += start_all(copies_of([corrected_v.at[s]], [direction.at[s]], more, 8 + s))
        wait_all(matrix_in[s])
        both = applied(jnp.concatenate(flat, axis=1), held[s], fine)
        for b in range(blocks):
            product_v[s, b] = both[:, b * width : (b + 1) * width]
        out += start_all(sends(product_v, table_s, outgoing, sems, s))
        out += start_all(copies_of([product_v.at[s]], [product.at[s]], more, 12 + s))
    out += start_all(rims(product_v, upward, downward, sems))
    wait_all(out)


def last_kernel(
    table, incoming, before, after, base, out, held, table_s, incoming_v, rims_v, sems, more
):
    subs, blocks = base.shape[:2]
    arriving = fetches(table, table_s, incoming, incoming_v, before, after, rims_v, sems)
    base_in = start_all(copies_of(parts_of(base), parts_of(held), more, 0))
    wait_all(arriving)
    leaving = []
    for s in range(subs):
        wait_all(base_in[s : s + 1])
        for b in range(blocks):
            held[s, b] = held[s, b] + received(table_s, incoming_v, rims_v, s, b)
        leaving += start_all(copies_of([held.at[s]], [out.at[s]], more, subs + s))
    wait_all(leaving)


def row_numbers(shape, rows_here, groups):
    row = lax.broadcasted_iota(jnp.int32, shape, 0)
    quarter = rows_here // groups
    return row // quarter * rows_here + row % quarter


def totals_kernel(rows_here, index_period, landed, index, totals):
    groups = index.shape[0]
    lanes = landed.shape[1]
    cases = lanes // groups
    period = index_period
    value = landed[...]
    row = lax.broadcasted_iota(jnp.int32, value.shape, 0)
    high, low = split(jnp.where(lax.rem(row, period) == period - 1, 0.0, value))
    rows = jnp.concatenate([high, low], axis=1)
    height = totals.shape[0]
    number = row_numbers((height, landed.shape[0]), rows_here, groups)
    lane = lax.broadcasted_iota(jnp.int32, (height, lanes), 1) // cases
    out = jnp.zeros((height, lanes), F32)
    for a in range(groups):
        gathered = jnp.zeros((height, lanes), F32)
        for q in range(groups):
            chosen = number == index[q : q + 1, :] - a * (rows_here // groups)
            product = dotted(jnp.where(chosen, 1.0, 0.0).astype(BF16), rows)
            gathered = jnp.where(lane == q, product[:, :lanes] + product[:, lanes:], gathered)
        summed = gathered
        for q in range(1, groups):
            summed = summed + pltpu.roll(gathered, q * cases, 1)
        out = jnp.where(lane == a, summed, out)
    totals[...] = out


def responses_kernel(rows_here, columns, index, responses):
    groups = index.shape[0]
    lanes = columns.shape[1]
    primal = lanes // groups
    high, low = split(columns[...].T)
    number = row_numbers((columns.shape[0], index.shape[1]), rows_here, groups)
    for q in range(groups):
        total = jnp.zeros((2 * primal, index.shape[1]), F32)
        for a in range(groups):
            chosen = number == index[q : q + 1, :] - a * (rows_here // groups)
            both = jnp.concatenate(
                [high[a * primal : (a + 1) * primal], low[a * primal : (a + 1) * primal]], axis=0
            )
            total = total + dotted(both, jnp.where(chosen, 1.0, 0.0).astype(BF16))
        responses[q * primal : (q + 1) * primal] = total[:primal].astype(BF16)
        responses[lanes + q * primal : lanes + (q + 1) * primal] = total[primal:].astype(BF16)


def all_to_all(block, axes):
    return lax.all_to_all(block, axes, split_axis=0, concat_axis=0, tiled=True)


def local(
    loads, schur, local_inverse, coarse_basis, coarse_inverse, primal_index, nbr_sub, nbr_block
):
    subs, blocks, cases, width = loads.shape
    coarse = primal_index.shape[1]
    primal = subs * coarse
    groups = subs
    faces = blocks - 2
    peers = lax.axis_size("sub")
    slabs = lax.axis_size("grp")
    devices = peers * slabs
    rows_here, prim_count = coarse_inverse.shape
    capacity = max(2, (subs * faces + peers - 2) // (peers - 1))
    period = coarse + 1
    size = blocks * width
    field_shape = loads.shape
    rim = (subs, cases, width)
    slot_shape = (peers, capacity * cases, width)
    face_sems = pltpu.SemaphoreType.DMA((subs, blocks))
    held_scratch = [pltpu.VMEM((subs, size, size), BF16), pltpu.SemaphoreType.DMA((subs, PIECES))]
    field_scratch = pltpu.VMEM(field_shape, F32)
    more_sems = pltpu.SemaphoreType.DMA((32,))
    field_bytes = 4 * subs * blocks * cases * width
    matrix_bytes = 2 * subs * size * size
    matrix_flops = 4 * subs * cases * size * size

    send_slots, recv_slots = face_routes(nbr_sub, nbr_block, peers, capacity)
    table = jnp.concatenate([nbr_sub, send_slots, recv_slots], axis=0)
    table = jnp.pad(table, ((0, 16 - 3 * subs), (0, width - blocks)))
    table_scratch = pltpu.SMEM(table.shape, jnp.int32)
    arrive_sems = pltpu.SemaphoreType.DMA((4,))
    rims_scratch = pltpu.VMEM((2, subs, cases, width), F32)
    slots_scratch = pltpu.VMEM((peers, capacity * cases, width), F32)
    up = [(i, i + 1) for i in range(slabs - 1)]
    down = [(j, i) for i, j in up]

    def exchange(outgoing, upward, downward):
        incoming = all_to_all(outgoing, "sub")
        before = lax.ppermute(upward, "grp", up)
        after = lax.ppermute(downward, "grp", down)
        return incoming, before, after

    def gather_rows(message):
        message = message.reshape(devices, period, 1, width)
        return all_to_all(message, AXES).reshape(devices * period, width)

    *packed, index_row = pl.pallas_call(
        pack_kernel,
        out_shape=(
            shape((peers, capacity * cases + 8, width)), shape(rim), shape(rim),
            shape((8, width)),
        ),
        in_specs=[SMEM, SMEM, VMEM],
        out_specs=(HBM, HBM, HBM, VMEM),
        scratch_shapes=[
            pltpu.VMEM((peers, 8, width), F32), face_sems, pltpu.SemaphoreType.DMA(())
        ],
        compiler_params=params(),
        cost_estimate=cost(0, 2 * field_bytes),
        name="pack",
    )(table, primal_index, loads)
    incoming, before, after = exchange(*packed)
    slab_index = incoming[:, capacity * cases, :primal].astype(jnp.int32).reshape(-1)

    flat_basis = coarse_basis.reshape(primal, size)
    basis_high = lax.reduce_precision(flat_basis, 8, 7)
    basis_low = flat_basis - basis_high
    basis = jnp.concatenate([basis_high, basis_low, basis_high, basis_low], axis=0).astype(BF16)

    def project(incoming, base, before, after, dots):
        return pl.pallas_call(
            functools.partial(project_kernel, len(dots)),
            out_shape=(shape(field_shape), shape((devices * period, width))),
            in_specs=[HBM] * (6 + len(dots)),
            out_specs=(HBM, HBM),
            scratch_shapes=[
                field_scratch,
                pltpu.VMEM((2 * subs * cases, size), BF16),
                pltpu.VMEM((2 * primal, size), BF16),
                pltpu.VMEM((width, width), F32),
                pltpu.VMEM((devices * period // 4, width), F32),
                table_scratch,
                pltpu.VMEM(incoming.shape, F32),
                rims_scratch,
                arrive_sems,
                more_sems,
            ],
            compiler_params=params(),
            cost_estimate=cost(8 * primal * subs * cases * size, 5 * field_bytes),
            name="project",
        )(table, incoming, before, after, base, basis, *dots)

    def inverse(field, fine):
        return pl.pallas_call(
            functools.partial(inverse_kernel, fine),
            out_shape=shape(field_shape),
            in_specs=[VMEM, HBM],
            out_specs=VMEM,
            scratch_shapes=held_scratch,
            compiler_params=params(),
            cost_estimate=cost(matrix_flops, matrix_bytes + 2 * field_bytes),
            name="inverse",
        )(field, local_inverse)

    def apply_schur(incoming, corrected, before, after, fine):
        return pl.pallas_call(
            functools.partial(schur_kernel, fine),
            out_shape=(
                shape(field_shape), shape(field_shape),
                shape(slot_shape), shape(rim), shape(rim),
            ),
            in_specs=[HBM] * 6,
            out_specs=(HBM,) * 5,
            scratch_shapes=[field_scratch] * 2
            + held_scratch
            + [table_scratch, slots_scratch, rims_scratch, arrive_sems, face_sems, more_sems],
            compiler_params=params(),
            cost_estimate=cost(matrix_flops, matrix_bytes + 6 * field_bytes),
            name="schur",
        )(
            table, incoming, before, after, corrected, schur,
        )

    def dot(a, b):
        return jnp.sum(a * b, axis=(0, 1))

    sent_shapes = (shape(slot_shape), shape(rim), shape(rim))
    sent_specs = (HBM, HBM, HBM)
    landed_scratch = pltpu.VMEM((devices * period, width), F32)
    responses_scratch = pltpu.VMEM((2 * groups * primal, devices * period), BF16)
    basis_scratch = pltpu.VMEM((4 * primal, size), BF16)
    combine_cost = cost(2 * primal * 8 * 128 * size, 8 * field_bytes)

    u0, message = project(incoming, loads, before, after, (index_row,))
    landed = gather_rows(message)

    columns_at = (
        jnp.arange(prim_count, dtype=jnp.int32)[:, None] == slab_index[None, :]
    ).astype(F32)
    asked = jnp.dot(coarse_inverse, columns_at, precision=PRECISE)
    asked = asked.reshape(groups, rows_here // groups, peers, primal).transpose(2, 1, 0, 3)
    asked = asked.reshape(peers, rows_here // groups, groups * primal)
    local0 = inverse(u0, False)
    asked, landed, local0 = lax.optimization_barrier((asked, landed, local0))
    columns = all_to_all(asked, "sub").reshape(-1, groups * primal)

    index = landed.reshape(devices, period, width)[:, coarse, :primal].astype(jnp.int32)
    index = index.reshape(devices, subs, coarse).transpose(1, 0, 2)
    index = jnp.pad(index, ((0, 0), (0, 0), (0, 1)), constant_values=-prim_count)
    index = index.reshape(subs, devices * period)
    height = prim_count // groups
    totals = pl.pallas_call(
        functools.partial(totals_kernel, rows_here, period),
        out_shape=shape((height, width)),
        in_specs=[VMEM, VMEM],
        out_specs=VMEM,
        compiler_params=params(),
        cost_estimate=cost(4 * prim_count * devices * period * groups * width, 2 * field_bytes),
        name="totals",
    )(landed, index)

    c0, *packed = pl.pallas_call(
        first_kernel,
        out_shape=(shape(field_shape),) + sent_shapes,
        in_specs=[HBM] * 5,
        out_specs=(HBM,) + sent_specs,
        scratch_shapes=[
            pltpu.VMEM((height, width), F32), pltpu.VMEM((height, width), F32), basis_scratch,
            field_scratch, field_scratch, table_scratch, face_sems, more_sems,
        ],
        compiler_params=params(),
        cost_estimate=combine_cost,
        name="first",
    )(table, columns, totals, basis, local0)
    incoming, before, after = exchange(*packed)
    responses = pl.pallas_call(
        functools.partial(responses_kernel, rows_here),
        out_shape=shape((2 * groups * primal, devices * period), BF16),
        in_specs=[VMEM, VMEM],
        out_specs=VMEM,
        compiler_params=params(),
        cost_estimate=cost(4 * primal * prim_count * devices * period * groups, field_bytes),
        name="responses",
    )(columns, index)
    dot0_part = dot(u0, c0)
    z0, q0, *packed = apply_schur(incoming, c0, before, after, False)
    incoming, before, after = exchange(*packed)

    v0, message = project(incoming, q0, before, after, (dot0_part, dot(z0, q0)))
    landed = gather_rows(message)
    local1 = inverse(v0, True)
    k0, c1, scalars, *packed = pl.pallas_call(
        second_kernel,
        out_shape=(
            shape(field_shape), shape(field_shape), shape((3, cases, width)),
        )
        + sent_shapes,
        in_specs=[HBM] * 6,
        out_specs=(HBM,) * 3 + sent_specs,
        scratch_shapes=[landed_scratch, responses_scratch, basis_scratch]
        + [field_scratch] * 3
        + [pltpu.VMEM((3, cases, width), F32), table_scratch, face_sems, more_sems],
        compiler_params=params(),
        cost_estimate=combine_cost,
        name="second",
    )(table, landed, responses, basis, local1, c0)
    incoming, before, after = exchange(*packed)
    dot1_part = dot(u0 - scalars[2] * v0, c1)
    z1, q1, *packed = apply_schur(incoming, c1, before, after, True)
    incoming, before, after = exchange(*packed)

    v1, message = project(incoming, q1, before, after, (dot1_part, dot(z1, q1), dot(z1, q0) + dot(z0, q1)))
    landed = gather_rows(message)
    local2 = inverse(v1, True)
    weighted, factors, *packed = pl.pallas_call(
        third_kernel,
        out_shape=(shape(field_shape), shape((2, cases, width))) + sent_shapes,
        in_specs=[HBM] * 8,
        out_specs=(HBM, HBM) + sent_specs,
        scratch_shapes=[
            landed_scratch, responses_scratch, basis_scratch, pltpu.VMEM((3, cases, width), F32)
        ]
        + [field_scratch] * 4
        + [pltpu.VMEM((2, cases, width), F32), table_scratch, face_sems, more_sems],
        compiler_params=params(),
        cost_estimate=combine_cost,
        name="third",
    )(table, landed, responses, basis, local2, k0, c1, scalars)
    incoming, before, after = exchange(*packed)
    result = factors[0] * z0 + factors[1] * z1
    precond = pl.pallas_call(
        last_kernel,
        out_shape=shape(field_shape),
        in_specs=[HBM] * 5,
        out_specs=HBM,
        scratch_shapes=[
            field_scratch, table_scratch, slots_scratch, rims_scratch, arrive_sems, more_sems
        ],
        compiler_params=params(),
        cost_estimate=cost(0, 4 * field_bytes),
        name="last",
    )(table, incoming, before, after, weighted)
    return (result, precond)


def solution(mesh):
    in_specs = (
        P(AXES, None, None, None),
        P(AXES, None, None),
        P(AXES, None, None),
        P(AXES, None, None, None),
        P("sub", None),
        P(AXES, None),
        P(AXES, None),
        P(AXES, None),
    )
    out_specs = (P(AXES, None, None, None), P(AXES, None, None, None))
    return jax.shard_map(local, mesh=mesh, in_specs=in_specs, out_specs=out_specs, check_vma=False)
```

```python
import functools

import jax
import jax.numpy as jnp
from jax import lax
from jax.experimental import pallas as pl
from jax.experimental.pallas import tpu as pltpu
from jax.sharding import PartitionSpec as P

AXES = ("grp", "sub")
PRECISE = lax.Precision.HIGHEST
F32 = jnp.float32
BF16 = jnp.bfloat16
SMEM = pl.BlockSpec(memory_space=pltpu.SMEM)
VMEM = pl.BlockSpec(memory_space=pltpu.VMEM)
HBM = pl.BlockSpec(memory_space=pltpu.HBM)
VMEM_LIMIT = 63 * 1024 * 1024
PIECES = 1
FACES = 6


def shape(dims, dtype=F32):
    return jax.ShapeDtypeStruct(dims, dtype)


def params(limit=VMEM_LIMIT):
    return pltpu.CompilerParams(vmem_limit_bytes=limit)


def cost(flops, moved):
    return pl.CostEstimate(flops=flops, bytes_accessed=moved, transcendentals=0)


def face_routes(nbr_sub, nbr_block, peer_count, capacity):
    subs, blocks = nbr_sub.shape
    face_count = blocks - 2
    shared = lax.broadcasted_iota(jnp.int32, nbr_sub.shape, 1) < face_count
    place = lax.broadcasted_iota(jnp.int32, nbr_sub.shape, 0) * face_count
    place = place + lax.broadcasted_iota(jnp.int32, nbr_sub.shape, 1)
    peer = jnp.where(shared, nbr_sub // subs % peer_count, -1)
    partner_place = nbr_sub % subs * face_count + nbr_block
    same = (peer[:, :, None, None] == peer[None, None]) & shared[None, None]

    def rank(order):
        return jnp.sum(same & (order[None, None] < order[:, :, None, None]), axis=(2, 3))

    first = jnp.maximum(peer, 0) * capacity
    return (first + rank(place), first + rank(partner_place))


def weight(table, s, b):
    return jnp.where(table[s, b] >= 0, 0.5, 1.0).astype(F32)


def split(x):
    high = x.astype(BF16)
    return high, (x - high.astype(F32)).astype(BF16)


def dotted(a, b):
    return lax.dot_general(a, b, (((1,), (0,)), ((), ())), preferred_element_type=F32)


def three_part(both, other):
    product = dotted(both, other)
    rows, columns = product.shape[0] // 2, product.shape[1] // 2
    return product[:rows, :columns] + product[:rows, columns:] + product[rows:, :columns]


def slot_of(buffer, slot, cases):
    capacity = buffer.shape[1] // cases
    start = pl.multiple_of(lax.rem(slot, capacity) * cases, cases)
    return buffer.at[lax.div(slot, capacity), pl.ds(start, cases)]


def sends(source, table, outgoing, sems, s):
    subs, blocks, cases = source.shape[:3]
    return [
        pltpu.make_async_copy(
            source.at[s, b], slot_of(outgoing, table[subs + s, b], cases), sems.at[s, b]
        )
        for b in range(blocks - 2)
    ]


def rims(source, upward, downward, sems):
    faces = source.shape[1] - 2
    return [
        pltpu.make_async_copy(source.at[:, faces], upward, sems.at[0, faces]),
        pltpu.make_async_copy(source.at[:, faces + 1], downward, sems.at[0, faces + 1]),
    ]


def fetches(table, table_s, incoming, incoming_v, before, after, rims_v, sems):
    return start_all(
        copies_of(
            [table, incoming, after, before],
            [table_s, incoming_v, rims_v.at[0], rims_v.at[1]], sems, 0,
        )
    )


def received(table_s, incoming_v, rims_v, s, b):
    subs, cases = rims_v.shape[1:3]
    faces = FACES
    if b >= faces:
        return rims_v[b - faces, s]
    slot = table_s[2 * subs + s, b]
    capacity = incoming_v.shape[1] // cases
    start = pl.multiple_of(lax.rem(slot, capacity) * cases, cases)
    return incoming_v[lax.div(slot, capacity), pl.ds(start, cases)]


def start_all(copies):
    for copy in copies:
        copy.start()
    return copies


def wait_all(copies):
    for copy in copies:
        copy.wait()


def copies_of(sources, targets, sems, first):
    return [
        pltpu.make_async_copy(source, target, sems.at[first + i])
        for i, (source, target) in enumerate(zip(sources, targets))
    ]


def parts_of(ref):
    return [ref.at[s] for s in range(ref.shape[0])]


def pack_kernel(
    table, primal, loads, outgoing, upward, downward, index_row, tall, sems, row_sem
):
    subs, blocks, cases, width = loads.shape
    coarse = primal.shape[1]
    copies = start_all(rims(loads, upward, downward, sems))
    for s in range(subs):
        copies += start_all(sends(loads, table, outgoing, sems, s))
    lane = lax.broadcasted_iota(jnp.int32, (1, width), 1)
    row = jnp.zeros((1, width), jnp.int32)
    for s in range(subs):
        for c in range(coarse):
            row = jnp.where(lane == s * coarse + c, primal[s, c], row)
    row = row.astype(F32)
    index_row[...] = jnp.broadcast_to(row, index_row.shape)
    tall[...] = jnp.broadcast_to(row[None], tall.shape)
    rows = outgoing.at[:, pl.ds(outgoing.shape[1] - tall.shape[1], tall.shape[1])]
    copies += start_all([pltpu.make_async_copy(tall, rows, row_sem)])
    wait_all(copies)


def project_kernel(
    dot_count, table, incoming, before, after, base, basis, *rest
):
    dots = rest[:dot_count]
    field, message, held, parts, factors, tall, block_rows = rest[dot_count : dot_count + 7]
    table_s, incoming_v, rims_v, sems, more = rest[dot_count + 7 :]
    subs, blocks, cases, width = base.shape
    lanes = subs * cases
    primal = basis.shape[0] // 4
    coarse = primal // subs
    arriving = fetches(table, table_s, incoming, incoming_v, before, after, rims_v, sems)
    base_in = start_all(copies_of(parts_of(base), parts_of(held), more, 0))
    others = [basis.at[pl.ds(0, 2 * primal)]]
    targets = [factors]
    place = 0
    for part in dots:
        others.append(part)
        targets.append(tall.at[pl.ds(place, part.shape[0])])
        place += part.shape[0]
    others = start_all(copies_of(others, targets, more, subs))
    tall[place:] = jnp.zeros((tall.shape[0] - place, width), F32)
    wait_all(arriving)
    out = []
    for s in range(subs):
        wait_all(base_in[s : s + 1])
        for b in range(blocks):
            other = received(table_s, incoming_v, rims_v, s, b)
            value = weight(table_s, s, b) * (held[s, b] + other)
            held[s, b] = value
            high, low = split(value)
            parts[s * cases : (s + 1) * cases, b * width : (b + 1) * width] = high
            parts[lanes + s * cases : lanes + (s + 1) * cases, b * width : (b + 1) * width] = low
        out += start_all(copies_of([held.at[s]], [field.at[s]], more, 8 + s))
    wait_all(others)
    product = lax.dot_general(
        factors[...], parts[...], (((1,), (1,)), ((), ())), preferred_element_type=F32
    )
    product = product[:primal, :lanes] + product[:primal, lanes:] + product[primal:, :lanes]
    lane = lax.broadcasted_iota(jnp.int32, (coarse, lanes), 1) // cases
    block = jnp.zeros((coarse, lanes), F32)
    for s in range(subs):
        block = jnp.where(lane == s, product[s * coarse : (s + 1) * coarse], block)
    if dot_count == 1:
        row = tall[0:1]
    else:
        row = jnp.sum(tall[...].T, axis=0, keepdims=True)
    period = coarse + 1
    height = block_rows.shape[0]
    for p in range(height // period):
        block_rows[p * period : p * period + coarse] = block
        block_rows[p * period + coarse : (p + 1) * period] = row
    count = message.shape[0] // height
    rows = [message.at[pl.ds(i * height, height)] for i in range(count)]
    out += start_all(copies_of([block_rows] * count, rows, more, 8 + subs))
    wait_all(out)


def applied(flat, matrix, fine):
    if not fine:
        return dotted(flat.astype(BF16), matrix)
    both = dotted(jnp.concatenate(split(flat), axis=0), matrix)
    return both[: flat.shape[0]] + both[flat.shape[0] :]


def pieces(matrix, held, sems):
    subs, rows = matrix.shape[:2]
    count = sems.shape[1]
    height = rows // count
    return [
        [
            pltpu.make_async_copy(
                matrix.at[s, pl.ds(i * height, height)],
                held.at[s, pl.ds(i * height, height)],
                sems.at[s, i],
            )
            for i in range(count)
        ]
        for s in range(subs)
    ]


def inverse_kernel(fine, field, matrix, out, held, sems):
    subs, blocks, cases, width = field.shape
    copies = [start_all(group) for group in pieces(matrix, held, sems)]
    for s in range(subs):
        flat = jnp.concatenate([field[s, b] for b in range(blocks)], axis=1)
        wait_all(copies[s])
        product = applied(flat, held[s], fine)
        for b in range(blocks):
            out[s, b] = product[:, b * width : (b + 1) * width]


def folded(product, primal):
    size = product.shape[0]
    turned = product.T
    row = lax.broadcasted_iota(jnp.int32, (size, size), 0) // primal
    lane = lax.broadcasted_iota(jnp.int32, (size, size), 1) // primal
    kept = jnp.where(row == lane, turned, 0.0)
    total = kept[:primal]
    for q in range(1, size // primal):
        total = total + kept[q * primal : (q + 1) * primal]
    out = total
    for q in range(1, size // primal):
        out = out + pltpu.roll(total, q * primal, 1)
    return out


def spread(picked, basis, subs, coarse):
    cases, lanes = picked.shape
    high = picked.astype(BF16).astype(F32)
    lane = lax.broadcasted_iota(jnp.int32, (cases, lanes), 1)
    parts = jnp.where(lane < lanes // 2, high, picked - high)
    owner = lane // coarse % subs
    tall = jnp.concatenate(
        [jnp.where(owner == s, parts, 0.0) for s in range(subs)], axis=0
    ).astype(BF16)
    return dotted(tall, basis[...])


def first_kernel(
    table, columns, totals, basis, local_part,
    corrected, outgoing, upward, downward,
    columns_v, totals_v, basis_v, local_v, weighted, table_s, sems, more,
):
    subs, blocks, cases, width = local_part.shape
    primal = basis.shape[0] // 4
    routes = start_all([pltpu.make_async_copy(table, table_s, sems.at[0, 0])])
    small = start_all(
        copies_of([columns, totals, basis], [columns_v, totals_v, basis_v], more, 0)
    )
    local_in = start_all(copies_of(parts_of(local_part), parts_of(local_v), more, 3))
    wait_all(small)
    wait_all(routes)
    high, low = split(columns_v[...].T)
    total_high, total_low = split(totals_v[...])
    product = three_part(
        jnp.concatenate([high, low], axis=0), jnp.concatenate([total_high, total_low], axis=1)
    )
    coarse_part = spread(folded(product, primal), basis_v, subs, primal // subs)
    out = []
    for s in range(subs):
        wait_all([local_in[s]])
        for b in range(blocks):
            value = local_v[s, b] + coarse_part[
                s * cases : (s + 1) * cases, b * width : (b + 1) * width
            ]
            local_v[s, b] = value
            weighted[s, b] = weight(table_s, s, b) * value
        out += start_all(sends(weighted, table_s, outgoing, sems, s))
        out += start_all(copies_of([local_v.at[s]], [corrected.at[s]], more, 3 + 2 * subs + s))
    out += start_all(rims(weighted, upward, downward, sems))
    wait_all(out)


def everyone(value, period):
    row = lax.broadcasted_iota(jnp.int32, value.shape, 0)
    sums = lax.rem(row, period) == period - 1
    totals = jnp.sum(jnp.where(sums, value, 0.0), axis=0, keepdims=True)
    totals = jnp.broadcast_to(totals, (value.shape[1], value.shape[1])).T
    high, low = split(jnp.where(sums, 0.0, value))
    return totals, jnp.concatenate([high, low], axis=1)


def second_kernel(
    table, landed, responses, basis, local_part, corrected,
    step_out, out_field, scalars, outgoing, upward, downward,
    landed_v, responses_v, basis_v, local_v, corrected_v, weighted, scalars_v, table_s, sems, more,
):
    subs, blocks, cases, width = corrected.shape
    primal = basis.shape[0] // 4
    coarse = primal // subs
    routes = start_all([pltpu.make_async_copy(table, table_s, sems.at[0, 0])])
    small = start_all(
        copies_of([landed, responses, basis], [landed_v, responses_v, basis_v], more, 0)
    )
    fields = [
        start_all(copies_of(parts_of(source), parts_of(target), more, 3 + i * subs))
        for i, (source, target) in enumerate(
            [(local_part, local_v), (corrected, corrected_v)]
        )
    ]
    wait_all(small)
    wait_all(routes)
    totals, rows = everyone(landed_v[...], coarse + 1)
    dot0 = totals[:cases]
    curv0 = totals[cases : 2 * cases]
    alpha = dot0 / curv0
    scalars_v[0] = dot0
    scalars_v[1] = curv0
    scalars_v[2] = alpha
    out = start_all(copies_of([scalars_v], [scalars], more, 3 + 6 * subs))
    product = three_part(responses_v[...], rows)
    coarse_part = spread(folded(product, primal), basis_v, subs, coarse)
    for s in range(subs):
        wait_all([group[s] for group in fields])
        for b in range(blocks):
            step = local_v[s, b] + coarse_part[
                s * cases : (s + 1) * cases, b * width : (b + 1) * width
            ]
            local_v[s, b] = step
            value = corrected_v[s, b] - alpha * step
            corrected_v[s, b] = value
            weighted[s, b] = weight(table_s, s, b) * value
        out += start_all(sends(weighted, table_s, outgoing, sems, s))
        out += start_all(
            copies_of(
                [local_v.at[s], corrected_v.at[s]], [step_out.at[s], out_field.at[s]],
                more, 3 + 4 * subs + 2 * s,
            )
        )
    out += start_all(rims(weighted, upward, downward, sems))
    wait_all(out)


def third_kernel(
    table, landed, responses, basis, local_part, older_step, corrected, scalars,
    weighted_out, factors, outgoing, upward, downward,
    landed_v, responses_v, basis_v, scalars_v, local_v, older_v, corrected_v, weighted,
    factors_v, table_s, sems, more,
):
    subs, blocks, cases, width = corrected.shape
    primal = basis.shape[0] // 4
    coarse = primal // subs
    routes = start_all([pltpu.make_async_copy(table, table_s, sems.at[0, 0])])
    small = start_all(
        copies_of(
            [landed, responses, basis, scalars],
            [landed_v, responses_v, basis_v, scalars_v], more, 0,
        )
    )
    fields = [
        start_all(copies_of(parts_of(source), parts_of(target), more, 4 + i * subs))
        for i, (source, target) in enumerate(
            [(local_part, local_v), (older_step, older_v), (corrected, corrected_v)]
        )
    ]
    wait_all(small)
    wait_all(routes)
    totals, rows = everyone(landed_v[...], coarse + 1)
    dot1 = totals[:cases]
    own = totals[cases : 2 * cases]
    cross = totals[2 * cases : 3 * cases]
    beta = dot1 / scalars_v[0]
    curv1 = own + beta * (cross + beta * scalars_v[1])
    alpha = dot1 / curv1
    factors_v[0] = scalars_v[2] + alpha * beta
    factors_v[1] = alpha
    out = start_all(copies_of([factors_v], [factors], more, 4 + 3 * subs))
    product = three_part(responses_v[...], rows)
    coarse_part = spread(folded(product, primal), basis_v, subs, coarse)
    for s in range(subs):
        wait_all([group[s] for group in fields])
        for b in range(blocks):
            step = local_v[s, b] + coarse_part[
                s * cases : (s + 1) * cases, b * width : (b + 1) * width
            ]
            value = corrected_v[s, b] - alpha * (step + beta * older_v[s, b])
            weighted[s, b] = weight(table_s, s, b) * value
        out += start_all(sends(weighted, table_s, outgoing, sems, s))
        out += start_all(
            copies_of([weighted.at[s]], [weighted_out.at[s]], more, 5 + 3 * subs + s)
        )
    out += start_all(rims(weighted, upward, downward, sems))
    wait_all(out)


def schur_kernel(
    fine, table, incoming, before, after, corrected, matrix,
    direction, product, outgoing, upward, downward,
    corrected_v, product_v, held, held_sems, table_s, incoming_v, rims_v, arrive_sems, sems, more,
):
    subs, blocks, cases, width = corrected.shape
    arriving = fetches(table, table_s, incoming, incoming_v, before, after, rims_v, arrive_sems)
    base_in = start_all(copies_of(parts_of(corrected), parts_of(corrected_v), more, 0))
    matrix_in = [start_all(group) for group in pieces(matrix, held, held_sems)]
    wait_all(arriving)
    out = []
    for s in range(subs):
        wait_all(base_in[s : s + 1])
        flat = []
        for b in range(blocks):
            other = received(table_s, incoming_v, rims_v, s, b)
            value = weight(table_s, s, b) * corrected_v[s, b] + other
            corrected_v[s, b] = value
            flat.append(value)
        out += start_all(copies_of([corrected_v.at[s]], [direction.at[s]], more, 8 + s))
        wait_all(matrix_in[s])
        both = applied(jnp.concatenate(flat, axis=1), held[s], fine)
        for b in range(blocks):
            product_v[s, b] = both[:, b * width : (b + 1) * width]
        out += start_all(sends(product_v, table_s, outgoing, sems, s))
        out += start_all(copies_of([product_v.at[s]], [product.at[s]], more, 12 + s))
    out += start_all(rims(product_v, upward, downward, sems))
    wait_all(out)


def last_kernel(
    table, incoming, before, after, base, out, held, table_s, incoming_v, rims_v, sems, more
):
    subs, blocks = base.shape[:2]
    arriving = fetches(table, table_s, incoming, incoming_v, before, after, rims_v, sems)
    base_in = start_all(copies_of(parts_of(base), parts_of(held), more, 0))
    wait_all(arriving)
    leaving = []
    for s in range(subs):
        wait_all(base_in[s : s + 1])
        for b in range(blocks):
            held[s, b] = held[s, b] + received(table_s, incoming_v, rims_v, s, b)
        leaving += start_all(copies_of([held.at[s]], [out.at[s]], more, subs + s))
    wait_all(leaving)


def row_numbers(shape, rows_here, groups):
    row = lax.broadcasted_iota(jnp.int32, shape, 0)
    quarter = rows_here // groups
    return row // quarter * rows_here + row % quarter


def totals_kernel(rows_here, period, landed, index, totals, landed_v, index_v, totals_v, sems):
    groups, width = index.shape
    height, lanes = totals.shape
    cases = lanes // groups
    quarter = rows_here // groups
    copies = start_all(copies_of([index, landed], [index_v, landed_v], sems, 0))
    copies[0].wait()
    unknowns = index_v[...]
    place = lax.div(unknowns, rows_here) * quarter + lax.rem(unknowns, quarter)
    place = jnp.where(unknowns >= 0, place, -1)
    group = lax.rem(lax.div(unknowns, quarter), groups)
    turned = jnp.concatenate([group, group], axis=0).astype(F32).T
    copies[1].wait()
    value = landed_v[...]
    row = lax.broadcasted_iota(jnp.int32, value.shape, 0)
    value = jnp.where(lax.rem(row, period) == period - 1, 0.0, value)
    rolled = [value] + [pltpu.roll(value, k * cases, 1) for k in range(1, groups)]
    lane = lax.broadcasted_iota(jnp.int32, value.shape, 1) // cases
    lane_value = lane.astype(F32)
    number = lax.broadcasted_iota(jnp.int32, (height, width), 0)
    out = jnp.zeros((height, lanes), F32)
    for q in range(groups):
        copied = rolled[(0 - q) % groups]
        for a in range(1, groups):
            copied = jnp.where(lane == a, rolled[(a - q) % groups], copied)
        copied = jnp.where(lane_value == turned[:, q : q + 1], copied, 0.0)
        chosen = jnp.where(number == place[q : q + 1, :], 1.0, 0.0).astype(BF16)
        product = dotted(chosen, jnp.concatenate(split(copied), axis=1))
        out = out + (product[:, :lanes] + product[:, lanes:])
    totals_v[...] = out
    wait_all(start_all(copies_of([totals_v], [totals], sems, 2)))


def responses_kernel(rows_here, columns, index, responses, columns_v, index_v, sems):
    groups = index.shape[0]
    lanes = columns.shape[1]
    primal = lanes // groups
    wait_all(start_all(copies_of([columns, index], [columns_v, index_v], sems, 0)))
    high, low = split(columns_v[...].T)
    number = row_numbers((columns.shape[0], index.shape[1]), rows_here, groups)
    for q in range(groups):
        total = jnp.zeros((2 * primal, index.shape[1]), F32)
        for a in range(groups):
            chosen = number == index_v[q : q + 1, :] - a * (rows_here // groups)
            both = jnp.concatenate(
                [high[a * primal : (a + 1) * primal], low[a * primal : (a + 1) * primal]], axis=0
            )
            total = total + dotted(both, jnp.where(chosen, 1.0, 0.0).astype(BF16))
        responses[q * primal : (q + 1) * primal] = total[:primal].astype(BF16)
        responses[lanes + q * primal : lanes + (q + 1) * primal] = total[primal:].astype(BF16)


def all_to_all(block, axes):
    return lax.all_to_all(block, axes, split_axis=0, concat_axis=0, tiled=True)


def local(
    loads, schur, local_inverse, coarse_basis, coarse_inverse, primal_index, nbr_sub, nbr_block
):
    subs, blocks, cases, width = loads.shape
    coarse = primal_index.shape[1]
    primal = subs * coarse
    groups = subs
    faces = blocks - 2
    peers = lax.axis_size("sub")
    slabs = lax.axis_size("grp")
    devices = peers * slabs
    rows_here, prim_count = coarse_inverse.shape
    capacity = max(2, (subs * faces + peers - 2) // (peers - 1))
    period = coarse + 1
    size = blocks * width
    field_shape = loads.shape
    rim = (subs, cases, width)
    slot_shape = (peers, capacity * cases, width)
    face_sems = pltpu.SemaphoreType.DMA((subs, blocks))
    held_scratch = [pltpu.VMEM((subs, size, size), BF16), pltpu.SemaphoreType.DMA((subs, PIECES))]
    field_scratch = pltpu.VMEM(field_shape, F32)
    more_sems = pltpu.SemaphoreType.DMA((32,))
    field_bytes = 4 * subs * blocks * cases * width
    matrix_bytes = 2 * subs * size * size
    matrix_flops = 4 * subs * cases * size * size

    send_slots, recv_slots = face_routes(nbr_sub, nbr_block, peers, capacity)
    table = jnp.concatenate([nbr_sub, send_slots, recv_slots], axis=0)
    table = jnp.pad(table, ((0, 16 - 3 * subs), (0, width - blocks)))
    table_scratch = pltpu.SMEM(table.shape, jnp.int32)
    arrive_sems = pltpu.SemaphoreType.DMA((4,))
    rims_scratch = pltpu.VMEM((2, subs, cases, width), F32)
    slots_scratch = pltpu.VMEM((peers, capacity * cases, width), F32)
    up = [(i, i + 1) for i in range(slabs - 1)]
    down = [(j, i) for i, j in up]

    def exchange(outgoing, upward, downward):
        incoming = all_to_all(outgoing, "sub")
        before = lax.ppermute(upward, "grp", up)
        after = lax.ppermute(downward, "grp", down)
        return incoming, before, after

    def gather_rows(message):
        message = message.reshape(devices, period, 1, width)
        return all_to_all(message, AXES).reshape(devices * period, width)

    *packed, index_row = pl.pallas_call(
        pack_kernel,
        out_shape=(
            shape((peers, capacity * cases + 8, width)), shape(rim), shape(rim),
            shape((8, width)),
        ),
        in_specs=[SMEM, SMEM, VMEM],
        out_specs=(HBM, HBM, HBM, VMEM),
        scratch_shapes=[
            pltpu.VMEM((peers, 8, width), F32), face_sems, pltpu.SemaphoreType.DMA(())
        ],
        compiler_params=params(),
        cost_estimate=cost(0, 2 * field_bytes),
        name="pack",
    )(table, primal_index, loads)
    incoming, before, after = exchange(*packed)
    slab_index = incoming[:, capacity * cases, :primal].astype(jnp.int32).reshape(-1)

    flat_basis = coarse_basis.reshape(primal, size)
    basis_high = lax.reduce_precision(flat_basis, 8, 7)
    basis_low = flat_basis - basis_high
    basis = jnp.concatenate([basis_high, basis_low, basis_high, basis_low], axis=0).astype(BF16)

    def project(incoming, base, before, after, dots):
        return pl.pallas_call(
            functools.partial(project_kernel, len(dots)),
            out_shape=(shape(field_shape), shape((devices * period, width))),
            in_specs=[HBM] * (6 + len(dots)),
            out_specs=(HBM, HBM),
            scratch_shapes=[
                field_scratch,
                pltpu.VMEM((2 * subs * cases, size), BF16),
                pltpu.VMEM((2 * primal, size), BF16),
                pltpu.VMEM((width, width), F32),
                pltpu.VMEM((devices * period // 4, width), F32),
                table_scratch,
                pltpu.VMEM(incoming.shape, F32),
                rims_scratch,
                arrive_sems,
                more_sems,
            ],
            compiler_params=params(),
            cost_estimate=cost(8 * primal * subs * cases * size, 5 * field_bytes),
            name="project",
        )(table, incoming, before, after, base, basis, *dots)

    def inverse(field, fine):
        return pl.pallas_call(
            functools.partial(inverse_kernel, fine),
            out_shape=shape(field_shape),
            in_specs=[VMEM, HBM],
            out_specs=VMEM,
            scratch_shapes=held_scratch,
            compiler_params=params(),
            cost_estimate=cost(matrix_flops, matrix_bytes + 2 * field_bytes),
            name="inverse",
        )(field, local_inverse)

    def apply_schur(incoming, corrected, before, after, fine):
        return pl.pallas_call(
            functools.partial(schur_kernel, fine),
            out_shape=(
                shape(field_shape), shape(field_shape),
                shape(slot_shape), shape(rim), shape(rim),
            ),
            in_specs=[HBM] * 6,
            out_specs=(HBM,) * 5,
            scratch_shapes=[field_scratch] * 2
            + held_scratch
            + [table_scratch, slots_scratch, rims_scratch, arrive_sems, face_sems, more_sems],
            compiler_params=params(),
            cost_estimate=cost(matrix_flops, matrix_bytes + 6 * field_bytes),
            name="schur",
        )(
            table, incoming, before, after, corrected, schur,
        )

    def dot(a, b):
        return jnp.sum(a * b, axis=(0, 1))

    sent_shapes = (shape(slot_shape), shape(rim), shape(rim))
    sent_specs = (HBM, HBM, HBM)
    index_scratch = pltpu.VMEM((subs, devices * period), jnp.int32)
    landed_scratch = pltpu.VMEM((devices * period, width), F32)
    responses_scratch = pltpu.VMEM((2 * groups * primal, devices * period), BF16)
    basis_scratch = pltpu.VMEM((4 * primal, size), BF16)
    combine_cost = cost(2 * primal * 8 * 128 * size, 8 * field_bytes)

    u0, message = project(incoming, loads, before, after, (index_row,))
    landed = gather_rows(message)

    columns_at = (
        jnp.arange(prim_count, dtype=jnp.int32)[:, None] == slab_index[None, :]
    ).astype(F32)
    asked = jnp.dot(coarse_inverse, columns_at, precision=PRECISE)
    asked = asked.reshape(groups, rows_here // groups, peers, primal).transpose(2, 1, 0, 3)
    asked = asked.reshape(peers, rows_here // groups, groups * primal)
    local0 = inverse(u0, False)
    asked, landed, local0 = lax.optimization_barrier((asked, landed, local0))
    columns = all_to_all(asked, "sub").reshape(-1, groups * primal)

    index = landed.reshape(devices, period, 1, width)[:, coarse, 0, :primal].astype(jnp.int32)
    index = index.reshape(devices, subs, coarse).transpose(1, 0, 2)
    index = jnp.pad(index, ((0, 0), (0, 0), (0, 1)), constant_values=-prim_count)
    index = index.reshape(subs, devices * period)
    height = prim_count // groups
    totals = pl.pallas_call(
        functools.partial(totals_kernel, rows_here, period),
        out_shape=shape((height, width)),
        in_specs=[HBM, HBM],
        out_specs=HBM,
        scratch_shapes=[
            landed_scratch, index_scratch, pltpu.VMEM((height, width), F32), arrive_sems
        ],
        compiler_params=params(),
        cost_estimate=cost(4 * prim_count * devices * period * width, 2 * field_bytes),
        name="totals",
    )(landed, index)

    c0, *packed = pl.pallas_call(
        first_kernel,
        out_shape=(shape(field_shape),) + sent_shapes,
        in_specs=[HBM] * 5,
        out_specs=(HBM,) + sent_specs,
        scratch_shapes=[
            pltpu.VMEM((height, width), F32), pltpu.VMEM((height, width), F32), basis_scratch,
            field_scratch, field_scratch, table_scratch, face_sems, more_sems,
        ],
        compiler_params=params(),
        cost_estimate=combine_cost,
        name="first",
    )(table, columns, totals, basis, local0)
    incoming, before, after = exchange(*packed)
    responses = pl.pallas_call(
        functools.partial(responses_kernel, rows_here),
        out_shape=shape((2 * groups * primal, devices * period), BF16),
        in_specs=[HBM, HBM],
        out_specs=VMEM,
        scratch_shapes=[pltpu.VMEM((height, width), F32), index_scratch, arrive_sems],
        compiler_params=params(),
        cost_estimate=cost(4 * primal * prim_count * devices * period * groups, field_bytes),
        name="responses",
    )(columns, index)
    dot0_part = dot(u0, c0)
    z0, q0, *packed = apply_schur(incoming, c0, before, after, False)
    incoming, before, after = exchange(*packed)

    v0, message = project(incoming, q0, before, after, (dot0_part, dot(z0, q0)))
    landed = gather_rows(message)
    local1 = inverse(v0, True)
    k0, c1, scalars, *packed = pl.pallas_call(
        second_kernel,
        out_shape=(
            shape(field_shape), shape(field_shape), shape((3, cases, width)),
        )
        + sent_shapes,
        in_specs=[HBM] * 6,
        out_specs=(HBM,) * 3 + sent_specs,
        scratch_shapes=[landed_scratch, responses_scratch, basis_scratch]
        + [field_scratch] * 3
        + [pltpu.VMEM((3, cases, width), F32), table_scratch, face_sems, more_sems],
        compiler_params=params(),
        cost_estimate=combine_cost,
        name="second",
    )(table, landed, responses, basis, local1, c0)
    incoming, before, after = exchange(*packed)
    dot1_part = dot(u0 - scalars[2] * v0, c1)
    z1, q1, *packed = apply_schur(incoming, c1, before, after, True)
    incoming, before, after = exchange(*packed)

    v1, message = project(incoming, q1, before, after, (dot1_part, dot(z1, q1), dot(z1, q0) + dot(z0, q1)))
    landed = gather_rows(message)
    local2 = inverse(v1, True)
    weighted, factors, *packed = pl.pallas_call(
        third_kernel,
        out_shape=(shape(field_shape), shape((2, cases, width))) + sent_shapes,
        in_specs=[HBM] * 8,
        out_specs=(HBM, HBM) + sent_specs,
        scratch_shapes=[
            landed_scratch, responses_scratch, basis_scratch, pltpu.VMEM((3, cases, width), F32)
        ]
        + [field_scratch] * 4
        + [pltpu.VMEM((2, cases, width), F32), table_scratch, face_sems, more_sems],
        compiler_params=params(),
        cost_estimate=combine_cost,
        name="third",
    )(table, landed, responses, basis, local2, k0, c1, scalars)
    incoming, before, after = exchange(*packed)
    result = factors[0] * z0 + factors[1] * z1
    precond = pl.pallas_call(
        last_kernel,
        out_shape=shape(field_shape),
        in_specs=[HBM] * 5,
        out_specs=HBM,
        scratch_shapes=[
            field_scratch, table_scratch, slots_scratch, rims_scratch, arrive_sems, more_sems
        ],
        compiler_params=params(),
        cost_estimate=cost(0, 4 * field_bytes),
        name="last",
    )(table, incoming, before, after, weighted)
    return (result, precond)


def solution(mesh):
    in_specs = (
        P(AXES, None, None, None),
        P(AXES, None, None),
        P(AXES, None, None),
        P(AXES, None, None, None),
        P("sub", None),
        P(AXES, None),
        P(AXES, None),
        P(AXES, None),
    )
    out_specs = (P(AXES, None, None, None), P(AXES, None, None, None))
    return jax.shard_map(local, mesh=mesh, in_specs=in_specs, out_specs=out_specs, check_vma=False)
```

```python
import functools

import jax
import jax.numpy as jnp
from jax import lax
from jax.experimental import pallas as pl
from jax.experimental.pallas import tpu as pltpu
from jax.sharding import PartitionSpec as P

AXES = ("grp", "sub")
PRECISE = lax.Precision.HIGHEST
F32 = jnp.float32
BF16 = jnp.bfloat16
SMEM = pl.BlockSpec(memory_space=pltpu.SMEM)
VMEM = pl.BlockSpec(memory_space=pltpu.VMEM)
HBM = pl.BlockSpec(memory_space=pltpu.HBM)
VMEM_LIMIT = 63 * 1024 * 1024
PIECES = 1
FACES = 6


def shape(dims, dtype=F32):
    return jax.ShapeDtypeStruct(dims, dtype)


def params(limit=VMEM_LIMIT):
    return pltpu.CompilerParams(vmem_limit_bytes=limit)


def cost(flops, moved):
    return pl.CostEstimate(flops=flops, bytes_accessed=moved, transcendentals=0)


def face_routes(nbr_sub, nbr_block, peer_count, capacity):
    subs, blocks = nbr_sub.shape
    face_count = blocks - 2
    shared = lax.broadcasted_iota(jnp.int32, nbr_sub.shape, 1) < face_count
    place = lax.broadcasted_iota(jnp.int32, nbr_sub.shape, 0) * face_count
    place = place + lax.broadcasted_iota(jnp.int32, nbr_sub.shape, 1)
    peer = jnp.where(shared, nbr_sub // subs % peer_count, -1)
    partner_place = nbr_sub % subs * face_count + nbr_block
    same = (peer[:, :, None, None] == peer[None, None]) & shared[None, None]

    def rank(order):
        return jnp.sum(same & (order[None, None] < order[:, :, None, None]), axis=(2, 3))

    first = jnp.maximum(peer, 0) * capacity
    return (first + rank(place), first + rank(partner_place))


def weight(table, s, b):
    return jnp.where(table[s, b] >= 0, 0.5, 1.0).astype(F32)


def split(x):
    high = x.astype(BF16)
    return high, (x - high.astype(F32)).astype(BF16)


def dotted(a, b):
    return lax.dot_general(a, b, (((1,), (0,)), ((), ())), preferred_element_type=F32)


def three_part(both, other):
    product = dotted(both, other)
    rows, columns = product.shape[0] // 2, product.shape[1] // 2
    return product[:rows, :columns] + product[:rows, columns:] + product[rows:, :columns]


def slot_of(buffer, slot, cases):
    capacity = buffer.shape[1] // cases
    start = pl.multiple_of(lax.rem(slot, capacity) * cases, cases)
    return buffer.at[lax.div(slot, capacity), pl.ds(start, cases)]


def sends(source, table, outgoing, sems, s):
    subs, blocks, cases = source.shape[:3]
    return [
        pltpu.make_async_copy(
            source.at[s, b], slot_of(outgoing, table[subs + s, b], cases), sems.at[s, b]
        )
        for b in range(blocks - 2)
    ]


def rims(source, upward, downward, sems):
    faces = source.shape[1] - 2
    return [
        pltpu.make_async_copy(source.at[:, faces], upward, sems.at[0, faces]),
        pltpu.make_async_copy(source.at[:, faces + 1], downward, sems.at[0, faces + 1]),
    ]


def fetches(table, table_s, incoming, incoming_v, before, after, rims_v, sems):
    return start_all(
        copies_of(
            [table, incoming, after, before],
            [table_s, incoming_v, rims_v.at[0], rims_v.at[1]], sems, 0,
        )
    )


def received(table_s, incoming_v, rims_v, s, b):
    subs, cases = rims_v.shape[1:3]
    faces = FACES
    if b >= faces:
        return rims_v[b - faces, s]
    slot = table_s[2 * subs + s, b]
    capacity = incoming_v.shape[1] // cases
    start = pl.multiple_of(lax.rem(slot, capacity) * cases, cases)
    return incoming_v[lax.div(slot, capacity), pl.ds(start, cases)]


def start_all(copies):
    for copy in copies:
        copy.start()
    return copies


def wait_all(copies):
    for copy in copies:
        copy.wait()


def copies_of(sources, targets, sems, first):
    return [
        pltpu.make_async_copy(source, target, sems.at[first + i])
        for i, (source, target) in enumerate(zip(sources, targets))
    ]


def parts_of(ref):
    return [ref.at[s] for s in range(ref.shape[0])]


def pack_kernel(
    table, primal, loads, outgoing, upward, downward, index_row, tall, sems, row_sem
):
    subs, blocks, cases, width = loads.shape
    coarse = primal.shape[1]
    copies = start_all(rims(loads, upward, downward, sems))
    for s in range(subs):
        copies += start_all(sends(loads, table, outgoing, sems, s))
    lane = lax.broadcasted_iota(jnp.int32, (1, width), 1)
    row = jnp.zeros((1, width), jnp.int32)
    for s in range(subs):
        for c in range(coarse):
            row = jnp.where(lane == s * coarse + c, primal[s, c], row)
    row = row.astype(F32)
    index_row[...] = jnp.broadcast_to(row, index_row.shape)
    tall[...] = jnp.broadcast_to(row[None], tall.shape)
    rows = outgoing.at[:, pl.ds(outgoing.shape[1] - tall.shape[1], tall.shape[1])]
    copies += start_all([pltpu.make_async_copy(tall, rows, row_sem)])
    wait_all(copies)


def project_kernel(
    dot_count, table, incoming, before, after, base, basis, *rest
):
    dots = rest[:dot_count]
    field, message, held, parts, factors, tall, block_rows = rest[dot_count : dot_count + 7]
    table_s, incoming_v, rims_v, sems, more = rest[dot_count + 7 :]
    subs, blocks, cases, width = base.shape
    lanes = subs * cases
    primal = basis.shape[0] // 4
    coarse = primal // subs
    arriving = fetches(table, table_s, incoming, incoming_v, before, after, rims_v, sems)
    base_in = start_all(copies_of(parts_of(base), parts_of(held), more, 0))
    others = [basis.at[pl.ds(0, 2 * primal)]]
    targets = [factors]
    place = 0
    for part in dots:
        others.append(part)
        targets.append(tall.at[pl.ds(place, part.shape[0])])
        place += part.shape[0]
    others = start_all(copies_of(others, targets, more, subs))
    tall[place:] = jnp.zeros((tall.shape[0] - place, width), F32)
    wait_all(arriving)
    out = []
    for s in range(subs):
        wait_all(base_in[s : s + 1])
        for b in range(blocks):
            other = received(table_s, incoming_v, rims_v, s, b)
            value = weight(table_s, s, b) * (held[s, b] + other)
            held[s, b] = value
            high, low = split(value)
            parts[s * cases : (s + 1) * cases, b * width : (b + 1) * width] = high
            parts[lanes + s * cases : lanes + (s + 1) * cases, b * width : (b + 1) * width] = low
        out += start_all(copies_of([held.at[s]], [field.at[s]], more, 8 + s))
    wait_all(others)
    product = lax.dot_general(
        factors[...], parts[...], (((1,), (1,)), ((), ())), preferred_element_type=F32
    )
    product = product[:primal, :lanes] + product[:primal, lanes:] + product[primal:, :lanes]
    lane = lax.broadcasted_iota(jnp.int32, (coarse, lanes), 1) // cases
    block = jnp.zeros((coarse, lanes), F32)
    for s in range(subs):
        block = jnp.where(lane == s, product[s * coarse : (s + 1) * coarse], block)
    if dot_count == 1:
        row = tall[0:1]
    else:
        row = jnp.sum(tall[...].T, axis=0, keepdims=True)
    period = coarse + 1
    height = block_rows.shape[0]
    for p in range(height // period):
        block_rows[p * period : p * period + coarse] = block
        block_rows[p * period + coarse : (p + 1) * period] = row
    count = message.shape[0] // height
    rows = [message.at[pl.ds(i * height, height)] for i in range(count)]
    out += start_all(copies_of([block_rows] * count, rows, more, 8 + subs))
    wait_all(out)


def applied(flat, matrix, fine):
    if not fine:
        return dotted(flat.astype(BF16), matrix)
    both = dotted(jnp.concatenate(split(flat), axis=0), matrix)
    return both[: flat.shape[0]] + both[flat.shape[0] :]


def pieces(matrix, held, sems):
    subs, rows = matrix.shape[:2]
    count = sems.shape[1]
    height = rows // count
    return [
        [
            pltpu.make_async_copy(
                matrix.at[s, pl.ds(i * height, height)],
                held.at[s, pl.ds(i * height, height)],
                sems.at[s, i],
            )
            for i in range(count)
        ]
        for s in range(subs)
    ]


def inverse_kernel(fine, field, matrix, out, held, sems):
    subs, blocks, cases, width = field.shape
    copies = [start_all(group) for group in pieces(matrix, held, sems)]
    for s in range(subs):
        flat = jnp.concatenate([field[s, b] for b in range(blocks)], axis=1)
        wait_all(copies[s])
        product = applied(flat, held[s], fine)
        for b in range(blocks):
            out[s, b] = product[:, b * width : (b + 1) * width]


def folded(product, primal):
    size = product.shape[0]
    turned = product.T
    row = lax.broadcasted_iota(jnp.int32, (size, size), 0) // primal
    lane = lax.broadcasted_iota(jnp.int32, (size, size), 1) // primal
    kept = jnp.where(row == lane, turned, 0.0)
    total = kept[:primal]
    for q in range(1, size // primal):
        total = total + kept[q * primal : (q + 1) * primal]
    out = total
    for q in range(1, size // primal):
        out = out + pltpu.roll(total, q * primal, 1)
    return out


def spread(picked, basis, subs, coarse):
    cases, lanes = picked.shape
    high = picked.astype(BF16).astype(F32)
    lane = lax.broadcasted_iota(jnp.int32, (cases, lanes), 1)
    parts = jnp.where(lane < lanes // 2, high, picked - high)
    owner = lane // coarse % subs
    tall = jnp.concatenate(
        [jnp.where(owner == s, parts, 0.0) for s in range(subs)], axis=0
    ).astype(BF16)
    return dotted(tall, basis[...])


def first_kernel(
    table, columns, totals, basis, local_part,
    corrected, outgoing, upward, downward,
    columns_v, totals_v, basis_v, local_v, weighted, table_s, sems, more,
):
    subs, blocks, cases, width = local_part.shape
    primal = basis.shape[0] // 4
    routes = start_all([pltpu.make_async_copy(table, table_s, sems.at[0, 0])])
    small = start_all(
        copies_of([columns, totals, basis], [columns_v, totals_v, basis_v], more, 0)
    )
    local_in = start_all(copies_of(parts_of(local_part), parts_of(local_v), more, 3))
    wait_all(small)
    wait_all(routes)
    high, low = split(columns_v[...].T)
    total_high, total_low = split(totals_v[...])
    product = three_part(
        jnp.concatenate([high, low], axis=0), jnp.concatenate([total_high, total_low], axis=1)
    )
    coarse_part = spread(folded(product, primal), basis_v, subs, primal // subs)
    out = []
    for s in range(subs):
        wait_all([local_in[s]])
        for b in range(blocks):
            value = local_v[s, b] + coarse_part[
                s * cases : (s + 1) * cases, b * width : (b + 1) * width
            ]
            local_v[s, b] = value
            weighted[s, b] = weight(table_s, s, b) * value
        out += start_all(sends(weighted, table_s, outgoing, sems, s))
        out += start_all(copies_of([local_v.at[s]], [corrected.at[s]], more, 3 + 2 * subs + s))
    out += start_all(rims(weighted, upward, downward, sems))
    wait_all(out)


def everyone(value, period):
    row = lax.broadcasted_iota(jnp.int32, value.shape, 0)
    sums = lax.rem(row, period) == period - 1
    totals = jnp.sum(jnp.where(sums, value, 0.0), axis=0, keepdims=True)
    totals = jnp.broadcast_to(totals, (value.shape[1], value.shape[1])).T
    high, low = split(jnp.where(sums, 0.0, value))
    return totals, jnp.concatenate([high, low], axis=1)


def second_kernel(
    table, landed, responses, basis, local_part, corrected,
    step_out, out_field, scalars, outgoing, upward, downward,
    landed_v, responses_v, basis_v, local_v, corrected_v, weighted, scalars_v, table_s, sems, more,
):
    subs, blocks, cases, width = corrected.shape
    primal = basis.shape[0] // 4
    coarse = primal // subs
    routes = start_all([pltpu.make_async_copy(table, table_s, sems.at[0, 0])])
    small = start_all(
        copies_of([landed, responses, basis], [landed_v, responses_v, basis_v], more, 0)
    )
    fields = [
        start_all(copies_of(parts_of(source), parts_of(target), more, 3 + i * subs))
        for i, (source, target) in enumerate(
            [(local_part, local_v), (corrected, corrected_v)]
        )
    ]
    wait_all(small)
    wait_all(routes)
    totals, rows = everyone(landed_v[...], coarse + 1)
    dot0 = totals[:cases]
    curv0 = totals[cases : 2 * cases]
    alpha = dot0 / curv0
    scalars_v[0] = dot0
    scalars_v[1] = curv0
    scalars_v[2] = alpha
    out = start_all(copies_of([scalars_v], [scalars], more, 3 + 6 * subs))
    product = three_part(responses_v[...], rows)
    coarse_part = spread(folded(product, primal), basis_v, subs, coarse)
    for s in range(subs):
        wait_all([group[s] for group in fields])
        for b in range(blocks):
            step = local_v[s, b] + coarse_part[
                s * cases : (s + 1) * cases, b * width : (b + 1) * width
            ]
            local_v[s, b] = step
            value = corrected_v[s, b] - alpha * step
            corrected_v[s, b] = value
            weighted[s, b] = weight(table_s, s, b) * value
        out += start_all(sends(weighted, table_s, outgoing, sems, s))
        out += start_all(
            copies_of(
                [local_v.at[s], corrected_v.at[s]], [step_out.at[s], out_field.at[s]],
                more, 3 + 4 * subs + 2 * s,
            )
        )
    out += start_all(rims(weighted, upward, downward, sems))
    wait_all(out)


def third_kernel(
    table, landed, responses, basis, local_part, older_step, corrected, scalars,
    weighted_out, factors, outgoing, upward, downward,
    landed_v, responses_v, basis_v, scalars_v, local_v, older_v, corrected_v, weighted,
    factors_v, table_s, sems, more,
):
    subs, blocks, cases, width = corrected.shape
    primal = basis.shape[0] // 4
    coarse = primal // subs
    routes = start_all([pltpu.make_async_copy(table, table_s, sems.at[0, 0])])
    small = start_all(
        copies_of(
            [landed, responses, basis, scalars],
            [landed_v, responses_v, basis_v, scalars_v], more, 0,
        )
    )
    fields = [
        start_all(copies_of(parts_of(source), parts_of(target), more, 4 + i * subs))
        for i, (source, target) in enumerate(
            [(local_part, local_v), (older_step, older_v), (corrected, corrected_v)]
        )
    ]
    wait_all(small)
    wait_all(routes)
    totals, rows = everyone(landed_v[...], coarse + 1)
    dot1 = totals[:cases]
    own = totals[cases : 2 * cases]
    cross = totals[2 * cases : 3 * cases]
    beta = dot1 / scalars_v[0]
    curv1 = own + beta * (cross + beta * scalars_v[1])
    alpha = dot1 / curv1
    factors_v[0] = scalars_v[2] + alpha * beta
    factors_v[1] = alpha
    out = start_all(copies_of([factors_v], [factors], more, 4 + 3 * subs))
    product = three_part(responses_v[...], rows)
    coarse_part = spread(folded(product, primal), basis_v, subs, coarse)
    for s in range(subs):
        wait_all([group[s] for group in fields])
        for b in range(blocks):
            step = local_v[s, b] + coarse_part[
                s * cases : (s + 1) * cases, b * width : (b + 1) * width
            ]
            value = corrected_v[s, b] - alpha * (step + beta * older_v[s, b])
            weighted[s, b] = weight(table_s, s, b) * value
        out += start_all(sends(weighted, table_s, outgoing, sems, s))
        out += start_all(
            copies_of([weighted.at[s]], [weighted_out.at[s]], more, 5 + 3 * subs + s)
        )
    out += start_all(rims(weighted, upward, downward, sems))
    wait_all(out)


def schur_kernel(
    fine, table, incoming, before, after, corrected, matrix,
    direction, product, outgoing, upward, downward,
    corrected_v, product_v, held, held_sems, table_s, incoming_v, rims_v, arrive_sems, sems, more,
):
    subs, blocks, cases, width = corrected.shape
    arriving = fetches(table, table_s, incoming, incoming_v, before, after, rims_v, arrive_sems)
    base_in = start_all(copies_of(parts_of(corrected), parts_of(corrected_v), more, 0))
    matrix_in = pieces(matrix, held, held_sems)
    for s, group in enumerate(matrix_in):
        for copy in group:
            copy.start(priority=s % 2)
    wait_all(arriving)
    out = []
    for s in range(subs):
        wait_all(base_in[s : s + 1])
        flat = []
        for b in range(blocks):
            other = received(table_s, incoming_v, rims_v, s, b)
            value = weight(table_s, s, b) * corrected_v[s, b] + other
            corrected_v[s, b] = value
            flat.append(value)
        out += start_all(copies_of([corrected_v.at[s]], [direction.at[s]], more, 8 + s))
        wait_all(matrix_in[s])
        both = applied(jnp.concatenate(flat, axis=1), held[s], fine)
        for b in range(blocks):
            product_v[s, b] = both[:, b * width : (b + 1) * width]
        out += start_all(sends(product_v, table_s, outgoing, sems, s))
        out += start_all(copies_of([product_v.at[s]], [product.at[s]], more, 12 + s))
    out += start_all(rims(product_v, upward, downward, sems))
    wait_all(out)


def last_kernel(
    table, incoming, before, after, base, out, held, table_s, incoming_v, rims_v, sems, more
):
    subs, blocks = base.shape[:2]
    arriving = fetches(table, table_s, incoming, incoming_v, before, after, rims_v, sems)
    base_in = start_all(copies_of(parts_of(base), parts_of(held), more, 0))
    wait_all(arriving)
    leaving = []
    for s in range(subs):
        wait_all(base_in[s : s + 1])
        for b in range(blocks):
            held[s, b] = held[s, b] + received(table_s, incoming_v, rims_v, s, b)
        leaving += start_all(copies_of([held.at[s]], [out.at[s]], more, subs + s))
    wait_all(leaving)


def row_numbers(shape, rows_here, groups):
    row = lax.broadcasted_iota(jnp.int32, shape, 0)
    quarter = rows_here // groups
    return row // quarter * rows_here + row % quarter


def totals_kernel(rows_here, period, landed, index, totals, landed_v, index_v, totals_v, sems):
    groups, width = index.shape
    height, lanes = totals.shape
    cases = lanes // groups
    quarter = rows_here // groups
    copies = start_all(copies_of([index, landed], [index_v, landed_v], sems, 0))
    copies[0].wait()
    unknowns = index_v[...]
    place = lax.div(unknowns, rows_here) * quarter + lax.rem(unknowns, quarter)
    place = jnp.where(unknowns >= 0, place, -1)
    group = lax.rem(lax.div(unknowns, quarter), groups)
    turned = jnp.concatenate([group, group], axis=0).astype(F32).T
    copies[1].wait()
    value = landed_v[...]
    row = lax.broadcasted_iota(jnp.int32, value.shape, 0)
    value = jnp.where(lax.rem(row, period) == period - 1, 0.0, value)
    rolled = [value] + [pltpu.roll(value, k * cases, 1) for k in range(1, groups)]
    lane = lax.broadcasted_iota(jnp.int32, value.shape, 1) // cases
    lane_value = lane.astype(F32)
    number = lax.broadcasted_iota(jnp.int32, (height, width), 0)
    out = jnp.zeros((height, lanes), F32)
    for q in range(groups):
        copied = rolled[(0 - q) % groups]
        for a in range(1, groups):
            copied = jnp.where(lane == a, rolled[(a - q) % groups], copied)
        copied = jnp.where(lane_value == turned[:, q : q + 1], copied, 0.0)
        chosen = jnp.where(number == place[q : q + 1, :], 1.0, 0.0).astype(BF16)
        product = dotted(chosen, jnp.concatenate(split(copied), axis=1))
        out = out + (product[:, :lanes] + product[:, lanes:])
    totals_v[...] = out
    wait_all(start_all(copies_of([totals_v], [totals], sems, 2)))


def responses_kernel(rows_here, columns, index, responses, columns_v, index_v, sems):
    groups = index.shape[0]
    lanes = columns.shape[1]
    primal = lanes // groups
    wait_all(start_all(copies_of([columns, index], [columns_v, index_v], sems, 0)))
    high, low = split(columns_v[...].T)
    number = row_numbers((columns.shape[0], index.shape[1]), rows_here, groups)
    for q in range(groups):
        total = jnp.zeros((2 * primal, index.shape[1]), F32)
        for a in range(groups):
            chosen = number == index_v[q : q + 1, :] - a * (rows_here // groups)
            both = jnp.concatenate(
                [high[a * primal : (a + 1) * primal], low[a * primal : (a + 1) * primal]], axis=0
            )
            total = total + dotted(both, jnp.where(chosen, 1.0, 0.0).astype(BF16))
        responses[q * primal : (q + 1) * primal] = total[:primal].astype(BF16)
        responses[lanes + q * primal : lanes + (q + 1) * primal] = total[primal:].astype(BF16)


def all_to_all(block, axes):
    return lax.all_to_all(block, axes, split_axis=0, concat_axis=0, tiled=True)


def local(
    loads, schur, local_inverse, coarse_basis, coarse_inverse, primal_index, nbr_sub, nbr_block
):
    subs, blocks, cases, width = loads.shape
    coarse = primal_index.shape[1]
    primal = subs * coarse
    groups = subs
    faces = blocks - 2
    peers = lax.axis_size("sub")
    slabs = lax.axis_size("grp")
    devices = peers * slabs
    rows_here, prim_count = coarse_inverse.shape
    capacity = max(2, (subs * faces + peers - 2) // (peers - 1))
    period = coarse + 1
    size = blocks * width
    field_shape = loads.shape
    rim = (subs, cases, width)
    slot_shape = (peers, capacity * cases, width)
    face_sems = pltpu.SemaphoreType.DMA((subs, blocks))
    held_scratch = [pltpu.VMEM((subs, size, size), BF16), pltpu.SemaphoreType.DMA((subs, PIECES))]
    field_scratch = pltpu.VMEM(field_shape, F32)
    more_sems = pltpu.SemaphoreType.DMA((32,))
    field_bytes = 4 * subs * blocks * cases * width
    matrix_bytes = 2 * subs * size * size
    matrix_flops = 4 * subs * cases * size * size

    send_slots, recv_slots = face_routes(nbr_sub, nbr_block, peers, capacity)
    table = jnp.concatenate([nbr_sub, send_slots, recv_slots], axis=0)
    table = jnp.pad(table, ((0, 16 - 3 * subs), (0, width - blocks)))
    table_scratch = pltpu.SMEM(table.shape, jnp.int32)
    arrive_sems = pltpu.SemaphoreType.DMA((4,))
    rims_scratch = pltpu.VMEM((2, subs, cases, width), F32)
    slots_scratch = pltpu.VMEM((peers, capacity * cases, width), F32)
    up = [(i, i + 1) for i in range(slabs - 1)]
    down = [(j, i) for i, j in up]

    def exchange(outgoing, upward, downward):
        incoming = all_to_all(outgoing, "sub")
        before = lax.ppermute(upward, "grp", up)
        after = lax.ppermute(downward, "grp", down)
        return incoming, before, after

    def gather_rows(message):
        message = message.reshape(devices, period, 1, width)
        return all_to_all(message, AXES).reshape(devices * period, width)

    *packed, index_row = pl.pallas_call(
        pack_kernel,
        out_shape=(
            shape((peers, capacity * cases + 8, width)), shape(rim), shape(rim),
            shape((8, width)),
        ),
        in_specs=[SMEM, SMEM, VMEM],
        out_specs=(HBM, HBM, HBM, VMEM),
        scratch_shapes=[
            pltpu.VMEM((peers, 8, width), F32), face_sems, pltpu.SemaphoreType.DMA(())
        ],
        compiler_params=params(),
        cost_estimate=cost(0, 2 * field_bytes),
        name="pack",
    )(table, primal_index, loads)
    incoming, before, after = exchange(*packed)
    slab_index = incoming[:, capacity * cases, :primal].astype(jnp.int32).reshape(-1)

    flat_basis = coarse_basis.reshape(primal, size)
    basis_high = lax.reduce_precision(flat_basis, 8, 7)
    basis_low = flat_basis - basis_high
    basis = jnp.concatenate([basis_high, basis_low, basis_high, basis_low], axis=0).astype(BF16)

    def project(incoming, base, before, after, dots):
        return pl.pallas_call(
            functools.partial(project_kernel, len(dots)),
            out_shape=(shape(field_shape), shape((devices * period, width))),
            in_specs=[HBM] * (6 + len(dots)),
            out_specs=(HBM, HBM),
            scratch_shapes=[
                field_scratch,
                pltpu.VMEM((2 * subs * cases, size), BF16),
                pltpu.VMEM((2 * primal, size), BF16),
                pltpu.VMEM((width, width), F32),
                pltpu.VMEM((devices * period // 4, width), F32),
                table_scratch,
                pltpu.VMEM(incoming.shape, F32),
                rims_scratch,
                arrive_sems,
                more_sems,
            ],
            compiler_params=params(),
            cost_estimate=cost(8 * primal * subs * cases * size, 5 * field_bytes),
            name="project",
        )(table, incoming, before, after, base, basis, *dots)

    def inverse(field, fine):
        return pl.pallas_call(
            functools.partial(inverse_kernel, fine),
            out_shape=shape(field_shape),
            in_specs=[VMEM, HBM],
            out_specs=VMEM,
            scratch_shapes=held_scratch,
            compiler_params=params(),
            cost_estimate=cost(matrix_flops, matrix_bytes + 2 * field_bytes),
            name="inverse",
        )(field, local_inverse)

    def apply_schur(incoming, corrected, before, after, fine):
        return pl.pallas_call(
            functools.partial(schur_kernel, fine),
            out_shape=(
                shape(field_shape), shape(field_shape),
                shape(slot_shape), shape(rim), shape(rim),
            ),
            in_specs=[HBM] * 6,
            out_specs=(HBM,) * 5,
            scratch_shapes=[field_scratch] * 2
            + held_scratch
            + [table_scratch, slots_scratch, rims_scratch, arrive_sems, face_sems, more_sems],
            compiler_params=params(),
            cost_estimate=cost(matrix_flops, matrix_bytes + 6 * field_bytes),
            name="schur",
        )(
            table, incoming, before, after, corrected, schur,
        )

    def dot(a, b):
        return jnp.sum(a * b, axis=(0, 1))

    sent_shapes = (shape(slot_shape), shape(rim), shape(rim))
    sent_specs = (HBM, HBM, HBM)
    index_scratch = pltpu.VMEM((subs, devices * period), jnp.int32)
    landed_scratch = pltpu.VMEM((devices * period, width), F32)
    responses_scratch = pltpu.VMEM((2 * groups * primal, devices * period), BF16)
    basis_scratch = pltpu.VMEM((4 * primal, size), BF16)
    combine_cost = cost(2 * primal * 8 * 128 * size, 8 * field_bytes)

    u0, message = project(incoming, loads, before, after, (index_row,))
    landed = gather_rows(message)

    columns_at = (
        jnp.arange(prim_count, dtype=jnp.int32)[:, None] == slab_index[None, :]
    ).astype(F32)
    asked = jnp.dot(coarse_inverse, columns_at, precision=PRECISE)
    asked = asked.reshape(groups, rows_here // groups, peers, primal).transpose(2, 1, 0, 3)
    asked = asked.reshape(peers, rows_here // groups, groups * primal)
    local0 = inverse(u0, False)
    asked, landed, local0 = lax.optimization_barrier((asked, landed, local0))
    columns = all_to_all(asked, "sub").reshape(-1, groups * primal)

    index = landed.reshape(devices, period, 1, width)[:, coarse, 0, :primal].astype(jnp.int32)
    index = index.reshape(devices, subs, coarse).transpose(1, 0, 2)
    index = jnp.pad(index, ((0, 0), (0, 0), (0, 1)), constant_values=-prim_count)
    index = index.reshape(subs, devices * period)
    height = prim_count // groups
    totals = pl.pallas_call(
        functools.partial(totals_kernel, rows_here, period),
        out_shape=shape((height, width)),
        in_specs=[HBM, HBM],
        out_specs=HBM,
        scratch_shapes=[
            landed_scratch, index_scratch, pltpu.VMEM((height, width), F32), arrive_sems
        ],
        compiler_params=params(),
        cost_estimate=cost(4 * prim_count * devices * period * width, 2 * field_bytes),
        name="totals",
    )(landed, index)

    c0, *packed = pl.pallas_call(
        first_kernel,
        out_shape=(shape(field_shape),) + sent_shapes,
        in_specs=[HBM] * 5,
        out_specs=(HBM,) + sent_specs,
        scratch_shapes=[
            pltpu.VMEM((height, width), F32), pltpu.VMEM((height, width), F32), basis_scratch,
            field_scratch, field_scratch, table_scratch, face_sems, more_sems,
        ],
        compiler_params=params(),
        cost_estimate=combine_cost,
        name="first",
    )(table, columns, totals, basis, local0)
    incoming, before, after = exchange(*packed)
    responses = pl.pallas_call(
        functools.partial(responses_kernel, rows_here),
        out_shape=shape((2 * groups * primal, devices * period), BF16),
        in_specs=[HBM, HBM],
        out_specs=VMEM,
        scratch_shapes=[pltpu.VMEM((height, width), F32), index_scratch, arrive_sems],
        compiler_params=params(),
        cost_estimate=cost(4 * primal * prim_count * devices * period * groups, field_bytes),
        name="responses",
    )(columns, index)
    dot0_part = dot(u0, c0)
    z0, q0, *packed = apply_schur(incoming, c0, before, after, False)
    incoming, before, after = exchange(*packed)

    v0, message = project(incoming, q0, before, after, (dot0_part, dot(z0, q0)))
    landed = gather_rows(message)
    local1 = inverse(v0, True)
    k0, c1, scalars, *packed = pl.pallas_call(
        second_kernel,
        out_shape=(
            shape(field_shape), shape(field_shape), shape((3, cases, width)),
        )
        + sent_shapes,
        in_specs=[HBM] * 6,
        out_specs=(HBM,) * 3 + sent_specs,
        scratch_shapes=[landed_scratch, responses_scratch, basis_scratch]
        + [field_scratch] * 3
        + [pltpu.VMEM((3, cases, width), F32), table_scratch, face_sems, more_sems],
        compiler_params=params(),
        cost_estimate=combine_cost,
        name="second",
    )(table, landed, responses, basis, local1, c0)
    incoming, before, after = exchange(*packed)
    dot1_part = dot(u0 - scalars[2] * v0, c1)
    z1, q1, *packed = apply_schur(incoming, c1, before, after, True)
    incoming, before, after = exchange(*packed)

    v1, message = project(incoming, q1, before, after, (dot1_part, dot(z1, q1), dot(z1, q0) + dot(z0, q1)))
    landed = gather_rows(message)
    local2 = inverse(v1, True)
    weighted, factors, *packed = pl.pallas_call(
        third_kernel,
        out_shape=(shape(field_shape), shape((2, cases, width))) + sent_shapes,
        in_specs=[HBM] * 8,
        out_specs=(HBM, HBM) + sent_specs,
        scratch_shapes=[
            landed_scratch, responses_scratch, basis_scratch, pltpu.VMEM((3, cases, width), F32)
        ]
        + [field_scratch] * 4
        + [pltpu.VMEM((2, cases, width), F32), table_scratch, face_sems, more_sems],
        compiler_params=params(),
        cost_estimate=combine_cost,
        name="third",
    )(table, landed, responses, basis, local2, k0, c1, scalars)
    incoming, before, after = exchange(*packed)
    result = factors[0] * z0 + factors[1] * z1
    precond = pl.pallas_call(
        last_kernel,
        out_shape=shape(field_shape),
        in_specs=[HBM] * 5,
        out_specs=HBM,
        scratch_shapes=[
            field_scratch, table_scratch, slots_scratch, rims_scratch, arrive_sems, more_sems
        ],
        compiler_params=params(),
        cost_estimate=cost(0, 4 * field_bytes),
        name="last",
    )(table, incoming, before, after, weighted)
    return (result, precond)


def solution(mesh):
    in_specs = (
        P(AXES, None, None, None),
        P(AXES, None, None),
        P(AXES, None, None),
        P(AXES, None, None, None),
        P("sub", None),
        P(AXES, None),
        P(AXES, None),
        P(AXES, None),
    )
    out_specs = (P(AXES, None, None, None), P(AXES, None, None, None))
    return jax.shard_map(local, mesh=mesh, in_specs=in_specs, out_specs=out_specs, check_vma=False)
```
